512 devices in a mesh: gx: 32 (over z, core), gy: 16 (over y, x).
Axes of the slice: x: 4, y: 4, z: 16, core: 2. Of those that a mesh axis runs over, the one named last changes fastest.
Arguments:
- source: float32 [256, 2048, 256], P('gx', 'gy'), may hold values from -8 to 8
- density: float32 [256, 2048, 256], P('gx', 'gy'), may hold values from 0.08 to 1.7
Outputs:
- pressure: float32 [256, 2048, 256], P('gx', 'gy')
- residual: float32 [256, 2048, 256], P('gx', 'gy')
The draws below stay inside these ranges and needn't reach their ends.
All inputs are finite; a program needn't handle non-finite values.
Results may differ from the reference program's by a relative error of at most 0.00021.
Values sent between devices are 32-bit elements; how exact they have to be, the bound alone decides.
A program may use at most 64 MiB of HBM per device.

```python
import math
import jax
import jax.numpy as jnp
from jax import lax

NZ = 256
ITERS = 2
NX = 256
NY = 2048


def grid_axes():
    x_axis = (jnp.arange(NX, dtype=jnp.float32) + 0.5) / NX
    y_axis = (jnp.arange(NY, dtype=jnp.float32) + 0.5) / NY
    z_axis = (jnp.arange(NZ, dtype=jnp.float32) + 0.5) / NZ
    return (x_axis, y_axis, z_axis)


def bump(axis_values, center, width):
    return jnp.exp(-0.5 * ((axis_values - center) / width) ** 2)


def draw_source(key, part):
    x_axis, y_axis, z_axis = grid_axes()
    two_pi = 2.0 * math.pi
    smooth = jnp.zeros((NX, NY, NZ), jnp.float32)
    mode_key = jax.random.fold_in(key, 11)
    for mode_index in range(6):
        numbers = jax.random.uniform(jax.random.fold_in(mode_key, mode_index), (7,), jnp.float32)
        wave_x = 0.5 + 3.5 * numbers[0]
        wave_y = 0.5 + 5.5 * numbers[1]
        wave_z = 2.0 * numbers[2]
        amplitude = 1.2 * numbers[6] - 0.6
        profile_x = jnp.cos(two_pi * (wave_x * x_axis + numbers[3]))
        profile_y = jnp.cos(two_pi * (wave_y * y_axis + numbers[4]))
        profile_z = jnp.cos(two_pi * (wave_z * z_axis + numbers[5]))
        smooth = smooth + amplitude * profile_x[:, None, None] * profile_y[None, :, None] * profile_z[None, None, :]
    plume_key = jax.random.fold_in(key, 23)
    for plume_index in range(5):
        numbers = jax.random.uniform(jax.random.fold_in(plume_key, plume_index), (5,), jnp.float32)
        strength = (1.0 + 1.5 * numbers[3]) * jnp.where(numbers[4] < 0.5, -1.0, 1.0)
        smooth = smooth + strength * bump(x_axis, numbers[0], 0.07)[:, None, None] * bump(y_axis, numbers[1], 0.07)[None, :, None] * bump(z_axis, 0.2 + 0.6 * numbers[2], 0.2)[None, None, :]
    noise_key = jax.random.fold_in(key, 37)
    rough = 0.35 * jnp.clip(jax.random.normal(noise_key, (NX, NY, NZ), jnp.float32), -4.0, 4.0)
    return jnp.clip(smooth + rough, -8.0, 8.0)


def draw_density(key, part):
    x_axis, y_axis, z_axis = grid_axes()
    two_pi = 2.0 * math.pi
    numbers = jax.random.uniform(jax.random.fold_in(key, 5), (6,), jnp.float32)
    height = 0.45 + 0.15 * numbers[0] + 0.08 * jnp.cos(two_pi * ((0.5 + 1.5 * numbers[1]) * x_axis + numbers[2]))[:, None] * jnp.cos(two_pi * ((0.5 + 1.5 * numbers[3]) * y_axis + numbers[4]))[None, :]
    layer = jax.nn.sigmoid((z_axis[None, None, :] - height[:, :, None]) / 0.06)
    columns = jnp.zeros((NX, NY), jnp.float32)
    column_key = jax.random.fold_in(key, 17)
    for column_index in range(4):
        picks = jax.random.uniform(jax.random.fold_in(column_key, column_index), (3,), jnp.float32)
        columns = columns + (1.0 + picks[2]) * bump(x_axis, picks[0], 0.06)[:, None] * bump(y_axis, picks[1], 0.06)[None, :]
    heat = 2.0 * layer + columns[:, :, None]
    noise_key = jax.random.fold_in(key, 29)
    rough = jax.random.uniform(noise_key, (NX, NY, NZ), jnp.float32, -0.5, 0.5)
    hotness = 1.0 - jnp.exp(-heat)
    log_mean = math.log(1.2) + hotness * math.log(1.0 / 6.0)
    spread = math.log(2.0) + hotness * math.log(3.0)
    return jnp.exp(log_mean + spread * rough)


def setup_inputs(seed: int = 0) -> dict:
    streams_of = jax.random.split(jax.random.key(seed), 3)
    source = draw_source(jax.random.fold_in(streams_of[2], 71), 0)
    density = draw_density(jax.random.fold_in(streams_of[2], 71), 0)
    return dict(source=source, density=density)


def neighbours(padded):
    return [padded[2:, 1:-1, 1:-1], padded[:-2, 1:-1, 1:-1], padded[1:-1, 2:, 1:-1], padded[1:-1, :-2, 1:-1], padded[1:-1, 1:-1, 2:], padded[1:-1, 1:-1, :-2]]

def face_weights(density):
    nearby = neighbours(jnp.pad(density, 1))
    weights = [2.0 / (density + other) for other in nearby]
    diag_sum = weights[0]
    for weight_one in weights[1:]:
        diag_sum = diag_sum + weight_one
    return (weights, lax.rsqrt(diag_sum))

def scaled_apply(field, weights, scale_inv):
    scaled = scale_inv * field
    nearby = neighbours(jnp.pad(scaled, 1))
    total = weights[0] * nearby[0]
    for weight_one, other in zip(weights[1:], nearby[1:]):
        total = total + weight_one * other
    return field - scale_inv * total

def reference(source, density):
    weights, scale_inv = face_weights(density)
    residual = scale_inv * source
    shadow = scaled_apply(residual, weights, scale_inv)
    solution = jnp.zeros_like(source)
    direction = jnp.zeros_like(source)
    along = jnp.zeros_like(source)
    pushed = jnp.zeros_like(source)
    gamma_old = jnp.float32(1.0)
    alpha_old = jnp.float32(1.0)
    for iteration in range(ITERS):
        gamma_now = jnp.sum(residual * residual)
        delta_now = jnp.sum(shadow * residual)
        fresh = scaled_apply(shadow, weights, scale_inv)
        if iteration == 0:
            beta_now = jnp.float32(0.0)
            alpha_now = gamma_now / delta_now
        else:
            beta_now = gamma_now / gamma_old
            alpha_now = gamma_now / (delta_now - beta_now * gamma_now / alpha_old)
        pushed = fresh + beta_now * pushed
        along = shadow + beta_now * along
        direction = residual + beta_now * direction
        solution = solution + alpha_now * direction
        residual = residual - alpha_now * along
        shadow = shadow - alpha_now * pushed
        gamma_old = gamma_now
        alpha_old = alpha_now
    return (scale_inv * solution, residual)
```

```python
import functools

import jax
import jax.numpy as jnp
from jax import lax
from jax.experimental import pallas as pl
from jax.experimental.pallas import tpu as pltpu
from jax.sharding import PartitionSpec as P

MESH = pl.DeviceIdType.MESH
F32 = jnp.float32
TOP = 16


def recip(x):
    r = pl.reciprocal(x, approx=True)
    return r * (2.0 - x * r)


def fold(v):
    rows, lanes = v.shape
    out = None
    for r in range(0, rows, 8):
        for c in range(0, lanes, 128):
            piece = v[r : r + 8, c : c + 128]
            out = piece if out is None else out + piece
    return out


def kernel(sizes, source, density, t1_out, t2_out, scale_out, coef_out,
           den, src, q0, q1, inv, wx, wy, wz, msg, got_y, got_x,
           local_sem, send_sem, recv_sem, sum_send, sum_recv):
    nx, ny = sizes
    depth, width, lanes = t1_out.shape
    end = TOP + width
    last = depth - 1
    i, j = lax.axis_index("gx"), lax.axis_index("gy")
    right, left = lax.rem(i + 1, nx), lax.rem(i + nx - 1, nx)
    above, below = lax.rem(j + 1, ny), lax.rem(j + ny - 1, ny)
    row_peers = [(i, lax.rem(j + k, ny)) for k in range(1, ny)]
    col_peers = [(lax.rem(i + k, nx), j) for k in range(1, nx)]
    corners = [(a, b) for a in (right, left) for b in (above, below)]

    body, low, high = pl.ds(TOP, width), pl.ds(TOP - 8, 8), pl.ds(end, 8)
    load_d = pltpu.make_async_copy(density, den.at[pl.ds(2, depth), body], local_sem.at[0])
    load_s = pltpu.make_async_copy(source, src.at[pl.ds(1, depth), body], local_sem.at[1])
    load_d.start()
    load_s.start()

    barrier = pltpu.get_barrier_semaphore()
    everyone = row_peers + col_peers + corners
    for peer in everyone:
        pl.semaphore_signal(barrier, inc=1, device_id=peer, device_id_type=MESH)
    pl.semaphore_wait(barrier, len(everyone))

    copies = []

    def send(what, where, peer):
        k = len(copies)
        copies.append(pltpu.make_async_remote_copy(
            src_ref=what, dst_ref=where, send_sem=send_sem.at[k], recv_sem=recv_sem.at[k],
            device_id=peer, device_id_type=MESH))
        return copies[-1]

    top_rows, first_rows = pl.ds(width - 8, 8), pl.ds(0, 8)
    own_d, own_s = pl.ds(2, depth), pl.ds(1, depth)
    rim_d = [
        send(density.at[:, top_rows], den.at[own_d, low], (i, above)),
        send(density.at[:, first_rows], den.at[own_d, high], (i, below)),
    ]
    face_d = [
        send(density.at[last], den.at[1, body], (right, j)),
        send(density.at[0], den.at[depth + 2, body], (left, j)),
    ]
    rim_s = [
        send(source.at[:, top_rows], src.at[own_s, low], (i, above)),
        send(source.at[:, first_rows], src.at[own_s, high], (i, below)),
    ]
    corner_d, corner_s = [], []
    for a in (right, left):
        plane, there = (last - 1, 0) if a is right else (0, depth + 2)
        face, face_there = (last, 0) if a is right else (0, depth + 1)
        for b, rows, place in ((above, top_rows, low), (below, first_rows, high)):
            corner_d.append(send(density.at[pl.ds(plane, 2), rows], den.at[pl.ds(there, 2), place], (a, b)))
            corner_s.append(send(source.at[face, rows], src.at[face_there, place], (a, b)))
    face_s = [
        send(source.at[last], src.at[0, body], (right, j)),
        send(source.at[0], src.at[depth + 1, body], (left, j)),
    ]
    second_d = [
        send(density.at[last - 1], den.at[0, body], (right, j)),
        send(density.at[1], den.at[depth + 3, body], (left, j)),
    ]
    for copy in copies:
        copy.start()
    field = [
        send(q0.at[last - 1 + 2, body], q0.at[0, body], (right, j)),
        send(q0.at[1 + 2, body], q0.at[depth + 3, body], (left, j)),
    ]

    def arrive(group):
        for copy in group:
            copy.wait_recv()

    mids = [(r, 16) for r in range(TOP, end, 16)]
    spans = [(TOP - 8, 8)] + mids + [(end, 8)]

    def keep_y(r, v):
        if r < TOP:
            return jnp.where(j > 0, v, 0.0)
        if r >= end:
            return jnp.where(j < ny - 1, v, 0.0)
        return v

    def faces_x(p):
        for r, n in spans:
            wx[p + 2, pl.ds(r, n)] = recip(den[p + 2, pl.ds(r, n)] + den[p + 3, pl.ds(r, n)])

    def inverse(p, keep=None, rim=True):
        for r, n in spans:
            d = den[p + 2, pl.ds(r, n)]
            lane = lax.broadcasted_iota(jnp.int32, (n, lanes), 1)
            up = recip(d + den[p + 2, pl.ds(r + 1, n)])
            wy[p + 1, pl.ds(r, n)] = up
            beyond = jnp.where(lane == lanes - 1, 0.0, pltpu.roll(d, lanes - 1, 1))
            ahead = recip(d + beyond)
            wz[p + 1, pl.ds(r, n)] = jnp.where(lane == lanes - 1, 0.0, ahead)
            behind = jnp.where(lane == 0, recip(d), pltpu.roll(ahead, 1, 1))
            diag = wx[p + 2, pl.ds(r, n)] + wx[p + 1, pl.ds(r, n)]
            diag = diag + up + wy[p + 1, pl.ds(r - 1, n)] + ahead + behind
            b = recip(diag)
            inv[p + 1, pl.ds(r, n)] = b
            if rim or TOP <= r < end:
                q = keep_y(r, b * src[p + 1, pl.ds(r, n)])
                if keep is not None:
                    q = jnp.where(keep, q, 0.0)
                q0[p + 2, pl.ds(r, n)] = q

    def rim_field(p):
        for r, n in (spans[0], spans[-1]):
            q0[p + 2, pl.ds(r, n)] = keep_y(r, inv[p + 1, pl.ds(r, n)] * src[p + 1, pl.ds(r, n)])

    def coupled(v, shift, p, r, n):
        mid = v[p + shift, pl.ds(r, n)]
        total = wx[p + 2, pl.ds(r, n)] * v[p + shift + 1, pl.ds(r, n)]
        total = total + wx[p + 1, pl.ds(r, n)] * v[p + shift - 1, pl.ds(r, n)]
        total = total + wy[p + 1, pl.ds(r, n)] * v[p + shift, pl.ds(r + 1, n)]
        total = total + wy[p + 1, pl.ds(r - 1, n)] * v[p + shift, pl.ds(r - 1, n)]
        w = wz[p + 1, pl.ds(r, n)]
        total = total + w * pltpu.roll(mid, lanes - 1, 1)
        return mid, total + pltpu.roll(w * mid, 1, 1)

    def first_apply(p, sums, keep=None, own=True):
        g0, d0, ss = sums
        for r, n in spans if own else mids:
            mid, total = coupled(q0, 2, p, r, n)
            s = src[p + 1, pl.ds(r, n)]
            t = s - total
            q = keep_y(r, inv[p + 1, pl.ds(r, n)] * t)
            if keep is not None:
                q = jnp.where(keep, q, 0.0)
            q1[p + 1, pl.ds(r, n)] = q
            if own and TOP <= r < end:
                t1_out[p, pl.ds(r - TOP, n)] = t
                g0 = g0 + fold(s * mid)
                d0 = d0 + fold(t * mid)
                ss = ss + fold(t * q)
        return g0, d0, ss

    def second_apply(p, h):
        for r, n in mids:
            mid, total = coupled(q1, 1, p, r, n)
            t = t1_out[p, pl.ds(r - TOP, n)] - total
            t2_out[p, pl.ds(r - TOP, n)] = t
            h = h + fold(t * mid)
        return h

    def over(start, step, count, f, carry=None):
        def go(k, c):
            return f(start + step * k, c)
        return lax.fori_loop(0, count, go, carry)

    def plain(f):
        def g(p, c):
            f(p)
            return c
        return g

    zero = jnp.zeros((8, 128), F32)
    load_d.wait()
    over(0, 1, last, plain(lambda p: [
        wx.__setitem__((p + 2, pl.ds(r, n)), recip(den[p + 2, pl.ds(r, n)] + den[p + 3, pl.ds(r, n)])) for r, n in mids]), 0)
    load_s.wait()
    arrive(rim_d)

    @pl.when(j == 0)
    def _():
        den[2 : depth + 2, TOP - 8 : TOP] = jnp.zeros((depth, 8, lanes), F32)

    @pl.when(j == ny - 1)
    def _():
        den[2 : depth + 2, end : end + 8] = jnp.zeros((depth, 8, lanes), F32)

    over(0, 1, last, plain(lambda p: [
        wx.__setitem__((p + 2, pl.ds(r, n)), recip(den[p + 2, pl.ds(r, n)] + den[p + 3, pl.ds(r, n)])) for r, n in (spans[0], spans[-1])]), 0)
    over(1, last - 2, 2, plain(lambda p: inverse(p, rim=False)), 0)
    for copy in field:
        copy.start()
    over(2, 1, depth - 4, plain(lambda p: inverse(p, rim=False)), 0)
    arrive(rim_s)
    over(1, 1, depth - 2, plain(rim_field), 0)
    sums = over(2, 1, depth - 4, first_apply, (zero, zero, zero))

    arrive(face_d)
    arrive(corner_d)
    for edge, first, there in ((0, i == 0, 0), (nx - 1, i == nx - 1, depth + 2)):
        @pl.when(first)
        def _():
            near = there + 1 if edge == 0 else there
            den[near, TOP - 8 : end + 8] = jnp.zeros((width + 16, lanes), F32)
    for bound, first, rows in ((0, j == 0, TOP - 8), (ny - 1, j == ny - 1, end)):
        @pl.when(first)
        def _():
            den[0:2, rows : rows + 8] = jnp.zeros((2, 8, lanes), F32)
            den[depth + 2 : depth + 4, rows : rows + 8] = jnp.zeros((2, 8, lanes), F32)

    over(-1, depth, 2, plain(faces_x), 0)
    arrive(corner_s)
    over(0, last, 2, plain(inverse), 0)
    sums = over(1, last - 2, 2, first_apply, sums)

    arrive(face_s)
    arrive(second_d)
    over(-2, depth + 2, 2, plain(faces_x), 0)

    def outer(p):
        return jnp.logical_or(jnp.logical_and(p < 0, i > 0), jnp.logical_and(p > 0, i < nx - 1))

    over(-1, depth + 1, 2, plain(lambda p: inverse(p, keep=outer(p))), 0)
    g0, d0, ss = over(0, last, 2, first_apply, sums)
    h = over(1, 1, depth - 2, second_apply, zero)

    arrive(field)
    over(-1, depth + 1, 2, plain(lambda p: first_apply(p, (None,) * 3, keep=outer(p), own=False)), 0)
    h = over(0, last, 2, second_apply, h)

    group = lax.broadcasted_iota(jnp.int32, (1, 128), 1) // 32
    row = jnp.zeros((1, 128), F32)
    for k, part in enumerate((g0, d0, ss, h)):
        v = jnp.sum(part, axis=0, keepdims=True)
        v = v + pltpu.roll(v, 64, 1)
        v = v + pltpu.roll(v, 32, 1)
        row = jnp.where(group == k, v, row)

    def spread(k, value, peers, got):
        msg[k] = value
        for s, peer in enumerate(peers):
            pltpu.make_async_remote_copy(
                src_ref=msg.at[k], dst_ref=got.at[s], send_sem=sum_send.at[k], recv_sem=sum_recv.at[k],
                device_id=peer, device_id_type=MESH).start()

    def gathered(k, value, got):
        pltpu.make_async_copy(got, got, sum_recv.at[k]).wait()
        for s in range(got.shape[0]):
            value = value + got[s]
        return value

    spread(0, row, row_peers, got_y)

    def scales(p):
        for r, n in mids:
            half = 0.5 * inv[p + 1, pl.ds(r, n)]
            scale_out[p, pl.ds(r - TOP, n)] = half * lax.rsqrt(half)

    over(0, 1, depth, plain(scales), 0)
    row = gathered(0, row, got_y)
    spread(1, row, col_peers, got_x)
    for copy in copies:
        copy.wait_send()
    row = gathered(1, row, got_x)
    pltpu.make_async_copy(got_y, got_y, sum_send.at[0]).wait()
    pltpu.make_async_copy(got_x, got_x, sum_send.at[1]).wait()

    def total(k):
        return jnp.broadcast_to(jnp.sum(jnp.where(group == k, row, 0.0), axis=1, keepdims=True), (1, 128))

    g0, d0, ss, h = (total(k) for k in range(4))
    alpha0 = g0 / d0
    gamma1 = g0 - 2.0 * alpha0 * d0 + alpha0 * alpha0 * ss
    delta1 = d0 - 2.0 * alpha0 * ss + alpha0 * alpha0 * h
    beta1 = gamma1 / g0
    alpha1 = gamma1 / (delta1 - beta1 * gamma1 / alpha0)
    coef_out[0:1] = alpha0 + alpha1 * (1.0 + beta1)
    coef_out[1:2] = alpha0 * alpha1


def solution(mesh):
    sizes = (mesh.shape["gx"], mesh.shape["gy"])

    def shards(source, density):
        depth, width, lanes = source.shape
        shape = jax.ShapeDtypeStruct(source.shape, F32)

        def planes(n):
            return pltpu.VMEM((n, TOP + width + 16, lanes), F32)

        vmem = pl.BlockSpec(memory_space=pltpu.VMEM)
        t1, t2, scale, coef = pl.pallas_call(
            functools.partial(kernel, sizes),
            out_shape=(shape, shape, shape, jax.ShapeDtypeStruct((2, 128), F32)),
            in_specs=[pl.BlockSpec(memory_space=pltpu.HBM)] * 2,
            out_specs=(vmem,) * 4,
            scratch_shapes=[
                planes(depth + 4), planes(depth + 2), planes(depth + 4), planes(depth + 2),
                planes(depth + 2), planes(depth + 3), planes(depth + 2), planes(depth + 2),
                pltpu.VMEM((2, 1, 128), F32),
                pltpu.VMEM((sizes[1] - 1, 1, 128), F32),
                pltpu.VMEM((sizes[0] - 1, 1, 128), F32),
                pltpu.SemaphoreType.DMA((2,)),
                pltpu.SemaphoreType.DMA((20,)),
                pltpu.SemaphoreType.DMA((20,)),
                pltpu.SemaphoreType.DMA((2,)),
                pltpu.SemaphoreType.DMA((2,)),
            ],
            compiler_params=pltpu.CompilerParams(
                collective_id=1, has_side_effects=True, vmem_limit_bytes=36 * 1024 * 1024),
        )(source, density)
        a, b = coef[0, 0], coef[1, 0]
        pressure = scale * scale * (a * source - b * t1)
        residual = scale * (source - a * t1 + b * t2)
        return pressure, residual

    spec = P("gx", "gy", None)
    return jax.shard_map(shards, mesh=mesh, in_specs=(spec, spec), out_specs=(spec, spec), check_vma=False)
```

```python
import functools

import jax
import jax.numpy as jnp
from jax import lax
from jax.experimental import pallas as pl
from jax.experimental.pallas import tpu as pltpu
from jax.sharding import PartitionSpec as P

MESH = pl.DeviceIdType.MESH
F32 = jnp.float32
TOP = 16


def recip(x):
    r = pl.reciprocal(x, approx=True)
    return r * (2.0 - x * r)


def fold(v):
    rows, lanes = v.shape
    out = None
    for r in range(0, rows, 8):
        for c in range(0, lanes, 128):
            piece = v[r : r + 8, c : c + 128]
            out = piece if out is None else out + piece
    return out


def kernel(sizes, source, density, t0_out, t1_out, t2_out, scale_out, coef_out,
           den, src, q0, q1, inv, wx, wy, wz, msg, got_y, got_x,
           local_sem, send_sem, recv_sem, sum_send, sum_recv):
    nx, ny = sizes
    depth, width, lanes = t1_out.shape
    end = TOP + width
    last = depth - 1
    i, j = lax.axis_index("gx"), lax.axis_index("gy")
    right, left = lax.rem(i + 1, nx), lax.rem(i + nx - 1, nx)
    above, below = lax.rem(j + 1, ny), lax.rem(j + ny - 1, ny)
    row_peers = [(i, lax.rem(j + k, ny)) for k in range(1, ny)]
    col_peers = [(lax.rem(i + k, nx), j) for k in range(1, nx)]
    corners = [(a, b) for a in (right, left) for b in (above, below)]

    body, low, high = pl.ds(TOP, width), pl.ds(TOP - 8, 8), pl.ds(end, 8)
    load_d = pltpu.make_async_copy(density, den.at[pl.ds(2, depth), body], local_sem.at[0])
    load_s = pltpu.make_async_copy(source, src.at[pl.ds(1, depth), body], local_sem.at[1])
    load_d.start()
    load_s.start()

    barrier = pltpu.get_barrier_semaphore()
    everyone = row_peers + col_peers + corners
    for peer in everyone:
        pl.semaphore_signal(barrier, inc=1, device_id=peer, device_id_type=MESH)
    pl.semaphore_wait(barrier, len(everyone))

    copies = []

    def send(what, where, peer):
        k = len(copies)
        copies.append(pltpu.make_async_remote_copy(
            src_ref=what, dst_ref=where, send_sem=send_sem.at[k], recv_sem=recv_sem.at[k],
            device_id=peer, device_id_type=MESH))
        return copies[-1]

    top_rows, first_rows = pl.ds(width - 8, 8), pl.ds(0, 8)
    own_d, own_s = pl.ds(2, depth), pl.ds(1, depth)
    rim_d = [
        send(density.at[:, top_rows], den.at[own_d, low], (i, above)),
        send(density.at[:, first_rows], den.at[own_d, high], (i, below)),
    ]
    face_d = [
        send(density.at[last], den.at[1, body], (right, j)),
        send(density.at[0], den.at[depth + 2, body], (left, j)),
    ]
    rim_s = [
        send(source.at[:, top_rows], src.at[own_s, low], (i, above)),
        send(source.at[:, first_rows], src.at[own_s, high], (i, below)),
    ]
    corner_d, corner_s = [], []
    for a in (right, left):
        plane, there = (last - 1, 0) if a is right else (0, depth + 2)
        face, face_there = (last, 0) if a is right else (0, depth + 1)
        for b, rows, place in ((above, top_rows, low), (below, first_rows, high)):
            corner_d.append(send(density.at[pl.ds(plane, 2), rows], den.at[pl.ds(there, 2), place], (a, b)))
            corner_s.append(send(source.at[face, rows], src.at[face_there, place], (a, b)))
    face_s = [
        send(source.at[last], src.at[0, body], (right, j)),
        send(source.at[0], src.at[depth + 1, body], (left, j)),
    ]
    second_d = [
        send(density.at[last - 1], den.at[0, body], (right, j)),
        send(density.at[1], den.at[depth + 3, body], (left, j)),
    ]
    for copy in copies:
        copy.start()
    field = [
        send(q0.at[last - 1 + 2, body], q0.at[0, body], (right, j)),
        send(q0.at[1 + 2, body], q0.at[depth + 3, body], (left, j)),
    ]

    def arrive(group):
        for copy in group:
            copy.wait_recv()

    mids = [(r, 16) for r in range(TOP, end, 16)]
    spans = [(TOP - 8, 8)] + mids + [(end, 8)]

    def keep_y(r, v):
        if r < TOP:
            return jnp.where(j > 0, v, 0.0)
        if r >= end:
            return jnp.where(j < ny - 1, v, 0.0)
        return v

    def faces_x(p, rows=spans):
        for r, n in rows:
            wx[p + 2, pl.ds(r, n)] = recip(den[p + 2, pl.ds(r, n)] + den[p + 3, pl.ds(r, n)])

    def inverse(p, keep=None, rim=True):
        for r, n in spans:
            d = den[p + 2, pl.ds(r, n)]
            lane = lax.broadcasted_iota(jnp.int32, (n, lanes), 1)
            up = recip(d + den[p + 2, pl.ds(r + 1, n)])
            wy[p + 1, pl.ds(r, n)] = up
            beyond = jnp.where(lane == lanes - 1, 0.0, pltpu.roll(d, lanes - 1, 1))
            ahead = recip(d + beyond)
            wz[p + 1, pl.ds(r, n)] = jnp.where(lane == lanes - 1, 0.0, ahead)
            behind = jnp.where(lane == 0, recip(d), pltpu.roll(ahead, 1, 1))
            diag = wx[p + 2, pl.ds(r, n)] + wx[p + 1, pl.ds(r, n)]
            diag = diag + up + wy[p + 1, pl.ds(r - 1, n)] + ahead + behind
            b = recip(diag)
            inv[p + 1, pl.ds(r, n)] = b
            if rim or TOP <= r < end:
                q = keep_y(r, b * src[p + 1, pl.ds(r, n)])
                if keep is not None:
                    q = jnp.where(keep, q, 0.0)
                q0[p + 2, pl.ds(r, n)] = q

    def rim_field(p):
        for r, n in (spans[0], spans[-1]):
            q0[p + 2, pl.ds(r, n)] = keep_y(r, inv[p + 1, pl.ds(r, n)] * src[p + 1, pl.ds(r, n)])

    def coupled(v, shift, p, r, n):
        mid = v[p + shift, pl.ds(r, n)]
        total = wx[p + 2, pl.ds(r, n)] * v[p + shift + 1, pl.ds(r, n)]
        total = total + wx[p + 1, pl.ds(r, n)] * v[p + shift - 1, pl.ds(r, n)]
        total = total + wy[p + 1, pl.ds(r, n)] * v[p + shift, pl.ds(r + 1, n)]
        total = total + wy[p + 1, pl.ds(r - 1, n)] * v[p + shift, pl.ds(r - 1, n)]
        w = wz[p + 1, pl.ds(r, n)]
        total = total + w * pltpu.roll(mid, lanes - 1, 1)
        return mid, total + pltpu.roll(w * mid, 1, 1)

    def first_apply(p, sums, keep=None, own=True):
        g0, d0, ss = sums
        for r, n in spans if own else mids:
            mid, total = coupled(q0, 2, p, r, n)
            s = src[p + 1, pl.ds(r, n)]
            t = s - total
            q = keep_y(r, inv[p + 1, pl.ds(r, n)] * t)
            if keep is not None:
                q = jnp.where(keep, q, 0.0)
            q1[p + 1, pl.ds(r, n)] = q
            if own and TOP <= r < end:
                t1_out[p, pl.ds(r - TOP, n)] = t
                g0 = g0 + fold(s * mid)
                d0 = d0 + fold(t * mid)
                ss = ss + fold(t * q)
        return g0, d0, ss

    def second_apply(p, h):
        for r, n in mids:
            mid, total = coupled(q1, 1, p, r, n)
            t = t1_out[p, pl.ds(r - TOP, n)] - total
            t2_out[p, pl.ds(r - TOP, n)] = t
            h = h + fold(t * mid)
        return h

    def over(start, step, count, f, carry=None):
        def go(k, c):
            return f(start + step * k, c)
        return lax.fori_loop(0, count, go, carry)

    def plain(f):
        def g(p, c):
            f(p)
            return c
        return g

    zero = jnp.zeros((8, 128), F32)
    load_d.wait()
    over(0, 1, last, plain(lambda p: faces_x(p, mids)), 0)
    load_s.wait()
    arrive(rim_d)

    @pl.when(j == 0)
    def _():
        den[2 : depth + 2, TOP - 8 : TOP] = jnp.zeros((depth, 8, lanes), F32)

    @pl.when(j == ny - 1)
    def _():
        den[2 : depth + 2, end : end + 8] = jnp.zeros((depth, 8, lanes), F32)

    over(0, 1, last, plain(lambda p: faces_x(p, (spans[0], spans[-1]))), 0)
    over(1, last - 2, 2, plain(lambda p: inverse(p, rim=False)), 0)
    for copy in field:
        copy.start()
    over(2, 1, depth - 4, plain(lambda p: inverse(p, rim=False)), 0)
    arrive(rim_s)
    over(1, 1, depth - 2, plain(rim_field), 0)
    sums = over(2, 1, depth - 4, first_apply, (zero, zero, zero))

    arrive(face_d)
    arrive(corner_d)
    for edge, first, there in ((0, i == 0, 0), (nx - 1, i == nx - 1, depth + 2)):
        @pl.when(first)
        def _():
            near = there + 1 if edge == 0 else there
            den[near, TOP - 8 : end + 8] = jnp.zeros((width + 16, lanes), F32)
    for bound, first, rows in ((0, j == 0, TOP - 8), (ny - 1, j == ny - 1, end)):
        @pl.when(first)
        def _():
            den[0:2, rows : rows + 8] = jnp.zeros((2, 8, lanes), F32)
            den[depth + 2 : depth + 4, rows : rows + 8] = jnp.zeros((2, 8, lanes), F32)

    over(-1, depth, 2, plain(faces_x), 0)
    arrive(corner_s)
    over(0, last, 2, plain(inverse), 0)
    sums = over(1, last - 2, 2, first_apply, sums)

    arrive(face_s)
    arrive(second_d)
    over(-2, depth + 2, 2, plain(faces_x), 0)

    def outer(p):
        return jnp.logical_or(jnp.logical_and(p < 0, i > 0), jnp.logical_and(p > 0, i < nx - 1))

    over(-1, depth + 1, 2, plain(lambda p: inverse(p, keep=outer(p))), 0)
    g0, d0, ss = over(0, last, 2, first_apply, sums)
    h = over(1, 1, depth - 2, second_apply, zero)

    arrive(field)
    over(-1, depth + 1, 2, plain(lambda p: first_apply(p, (None,) * 3, keep=outer(p), own=False)), 0)
    h = over(0, last, 2, second_apply, h)

    group = lax.broadcasted_iota(jnp.int32, (1, 128), 1) // 32
    row = jnp.zeros((1, 128), F32)
    for k, part in enumerate((g0, d0, ss, h)):
        v = jnp.sum(part, axis=0, keepdims=True)
        v = v + pltpu.roll(v, 64, 1)
        v = v + pltpu.roll(v, 32, 1)
        row = jnp.where(group == k, v, row)

    def spread(k, value, peers, got):
        msg[k] = value
        for s, peer in enumerate(peers):
            pltpu.make_async_remote_copy(
                src_ref=msg.at[k], dst_ref=got.at[s], send_sem=sum_send.at[k], recv_sem=sum_recv.at[k],
                device_id=peer, device_id_type=MESH).start()

    def gathered(k, value, got):
        pltpu.make_async_copy(got, got, sum_recv.at[k]).wait()
        for s in range(got.shape[0]):
            value = value + got[s]
        return value

    spread(0, row, row_peers, got_y)

    def scales(p):
        for r, n in mids:
            rows = pl.ds(r - TOP, n)
            half = 0.5 * inv[p + 1, pl.ds(r, n)]
            scale = half * lax.rsqrt(half)
            scale_out[p, rows] = scale
            t0_out[p, rows] = scale * src[p + 1, pl.ds(r, n)]
            t1_out[p, rows] = scale * t1_out[p, rows]
            t2_out[p, rows] = scale * t2_out[p, rows]

    over(0, 1, depth, plain(scales), 0)
    row = gathered(0, row, got_y)
    spread(1, row, col_peers, got_x)
    for copy in copies:
        copy.wait_send()
    row = gathered(1, row, got_x)
    pltpu.make_async_copy(got_y, got_y, sum_send.at[0]).wait()
    pltpu.make_async_copy(got_x, got_x, sum_send.at[1]).wait()

    def total(k):
        return jnp.broadcast_to(jnp.sum(jnp.where(group == k, row, 0.0), axis=1, keepdims=True), (1, 128))

    g0, d0, ss, h = (total(k) for k in range(4))
    alpha0 = g0 / d0
    gamma1 = g0 - 2.0 * alpha0 * d0 + alpha0 * alpha0 * ss
    delta1 = d0 - 2.0 * alpha0 * ss + alpha0 * alpha0 * h
    beta1 = gamma1 / g0
    alpha1 = gamma1 / (delta1 - beta1 * gamma1 / alpha0)
    coef_out[0:1] = alpha0 + alpha1 * (1.0 + beta1)
    coef_out[1:2] = alpha0 * alpha1


def combine(t0, t1, t2, scale, coef, pressure, residual, held_p, held_r, sem):
    a, b = coef[0:1, 0:1], coef[1:2, 0:1]
    copies = []
    for p in range(t0.shape[0]):
        u0, u1 = t0[p], t1[p]
        held_p[p] = scale[p] * (a * u0 - b * u1)
        held_r[p] = u0 - a * u1 + b * t2[p]
        for k, (held, out) in enumerate(((held_p, pressure), (held_r, residual))):
            copies.append(pltpu.make_async_copy(held.at[p], out.at[p], sem.at[k, p]))
            copies[-1].start()
    for copy in copies:
        copy.wait()


def solution(mesh):
    sizes = (mesh.shape["gx"], mesh.shape["gy"])

    def shards(source, density):
        depth, width, lanes = source.shape
        shape = jax.ShapeDtypeStruct(source.shape, F32)

        def planes(n):
            return pltpu.VMEM((n, TOP + width + 16, lanes), F32)

        vmem = pl.BlockSpec(memory_space=pltpu.VMEM)
        hbm = pl.BlockSpec(memory_space=pltpu.HBM)
        t0, t1, t2, scale, coef = pl.pallas_call(
            functools.partial(kernel, sizes),
            out_shape=(shape,) * 4 + (jax.ShapeDtypeStruct((2, 128), F32),),
            in_specs=[hbm] * 2,
            out_specs=(vmem,) * 5,
            scratch_shapes=[
                planes(depth + 4), planes(depth + 2), planes(depth + 4), planes(depth + 2),
                planes(depth + 2), planes(depth + 3), planes(depth + 2), planes(depth + 2),
                pltpu.VMEM((2, 1, 128), F32),
                pltpu.VMEM((sizes[1] - 1, 1, 128), F32),
                pltpu.VMEM((sizes[0] - 1, 1, 128), F32),
                pltpu.SemaphoreType.DMA((2,)),
                pltpu.SemaphoreType.DMA((20,)),
                pltpu.SemaphoreType.DMA((20,)),
                pltpu.SemaphoreType.DMA((2,)),
                pltpu.SemaphoreType.DMA((2,)),
            ],
            compiler_params=pltpu.CompilerParams(
                collective_id=1, has_side_effects=True, vmem_limit_bytes=36 * 1024 * 1024),
        )(pltpu.with_memory_space_constraint(source, pltpu.HBM), pltpu.with_memory_space_constraint(density, pltpu.HBM))
        pressure, residual = pl.pallas_call(
            combine,
            out_shape=(shape, shape),
            in_specs=[vmem] * 5,
            out_specs=(hbm, hbm),
            scratch_shapes=[
                pltpu.VMEM(source.shape, F32), pltpu.VMEM(source.shape, F32), pltpu.SemaphoreType.DMA((2, depth))],
            compiler_params=pltpu.CompilerParams(vmem_limit_bytes=16 * 1024 * 1024),
        )(t0, t1, t2, scale, coef)
        return pressure, residual

    spec = P("gx", "gy", None)
    return jax.shard_map(shards, mesh=mesh, in_specs=(spec, spec), out_specs=(spec, spec), check_vma=False)
```

```python
import functools

import jax
import jax.numpy as jnp
from jax import lax
from jax.experimental import pallas as pl
from jax.experimental.pallas import tpu as pltpu
from jax.sharding import PartitionSpec as P

MESH = pl.DeviceIdType.MESH
F32 = jnp.float32
TOP = 16


def recip(x):
    r = pl.reciprocal(x, approx=True)
    return r * (2.0 - x * r)


def fold(v):
    rows, lanes = v.shape
    out = None
    for r in range(0, rows, 8):
        for c in range(0, lanes, 128):
            piece = v[r : r + 8, c : c + 128]
            out = piece if out is None else out + piece
    return out


def kernel(sizes, source, density, t0_out, t1_out, t2_out, scale_out, coef_out,
           den, src, q0, q1, inv, wx, wy, wz, msg, got_y, got_x,
           local_sem, send_sem, recv_sem, sum_send, sum_recv, known):
    nx, ny = sizes
    depth, width, lanes = t1_out.shape
    end = TOP + width
    last = depth - 1
    i, j = lax.axis_index("gx"), lax.axis_index("gy")
    right, left = lax.rem(i + 1, nx), lax.rem(i + nx - 1, nx)
    above, below = lax.rem(j + 1, ny), lax.rem(j + ny - 1, ny)
    row_peers = [(i, lax.rem(j + k, ny)) for k in range(1, ny)]
    col_peers = [(lax.rem(i + k, nx), j) for k in range(1, nx)]
    corners = [(a, b) for a in (right, left) for b in (above, below)]

    body, low, high = pl.ds(TOP, width), pl.ds(TOP - 8, 8), pl.ds(end, 8)
    load_d = pltpu.make_async_copy(density, den.at[pl.ds(2, depth), body], local_sem.at[0])
    load_s = pltpu.make_async_copy(source, src.at[pl.ds(1, depth), body], local_sem.at[1])
    load_d.start()
    load_s.start()

    barrier = pltpu.get_barrier_semaphore()
    rounds = (nx - 1).bit_length() - 1
    nearby = [(right, j), (left, j)] + corners + row_peers
    for peer in nearby:
        pl.semaphore_signal(barrier, inc=1, device_id=peer, device_id_type=MESH)
    pl.semaphore_wait(barrier, len(nearby))

    def tell(k):
        if k >= rounds:
            return
        for step in (2**k, nx - 2**k):
            pl.semaphore_signal(known.at[k], inc=1, device_id=(lax.rem(i + step, nx), j), device_id_type=MESH)

    def heard(k):
        if k < rounds:
            pl.semaphore_wait(known.at[k], 2)

    copies = []

    def send(what, where, peer):
        k = len(copies)
        copies.append(pltpu.make_async_remote_copy(
            src_ref=what, dst_ref=where, send_sem=send_sem.at[k], recv_sem=recv_sem.at[k],
            device_id=peer, device_id_type=MESH))
        return copies[-1]

    top_rows, first_rows = pl.ds(width - 8, 8), pl.ds(0, 8)
    own_d, own_s = pl.ds(2, depth), pl.ds(1, depth)
    rim_d = [
        send(density.at[:, top_rows], den.at[own_d, low], (i, above)),
        send(density.at[:, first_rows], den.at[own_d, high], (i, below)),
    ]
    face_d = [
        send(density.at[last], den.at[1, body], (right, j)),
        send(density.at[0], den.at[depth + 2, body], (left, j)),
    ]
    rim_s = [
        send(source.at[:, top_rows], src.at[own_s, low], (i, above)),
        send(source.at[:, first_rows], src.at[own_s, high], (i, below)),
    ]
    corner_d, corner_s = [], []
    for a in (right, left):
        plane, there = (last - 1, 0) if a is right else (0, depth + 2)
        face, face_there = (last, 0) if a is right else (0, depth + 1)
        for b, rows, place in ((above, top_rows, low), (below, first_rows, high)):
            corner_d.append(send(density.at[pl.ds(plane, 2), rows], den.at[pl.ds(there, 2), place], (a, b)))
            corner_s.append(send(source.at[face, rows], src.at[face_there, place], (a, b)))
    face_s = [
        send(source.at[last], src.at[0, body], (right, j)),
        send(source.at[0], src.at[depth + 1, body], (left, j)),
    ]
    second_d = [
        send(density.at[last - 1], den.at[0, body], (right, j)),
        send(density.at[1], den.at[depth + 3, body], (left, j)),
    ]
    for copy in copies:
        copy.start()
    field = [
        send(q0.at[last - 1 + 2, body], q0.at[0, body], (right, j)),
        send(q0.at[1 + 2, body], q0.at[depth + 3, body], (left, j)),
    ]

    def arrive(group):
        for copy in group:
            copy.wait_recv()

    mids = [(r, 16) for r in range(TOP, end, 16)]
    spans = [(TOP - 8, 8)] + mids + [(end, 8)]

    def keep_y(r, v):
        if r < TOP:
            return jnp.where(j > 0, v, 0.0)
        if r >= end:
            return jnp.where(j < ny - 1, v, 0.0)
        return v

    def faces_x(p, rows=spans):
        for r, n in rows:
            wx[p + 2, pl.ds(r, n)] = recip(den[p + 2, pl.ds(r, n)] + den[p + 3, pl.ds(r, n)])

    def inverse(p, keep=None, rim=True):
        for r, n in spans:
            d = den[p + 2, pl.ds(r, n)]
            lane = lax.broadcasted_iota(jnp.int32, (n, lanes), 1)
            up = recip(d + den[p + 2, pl.ds(r + 1, n)])
            wy[p + 1, pl.ds(r, n)] = up
            beyond = jnp.where(lane == lanes - 1, 0.0, pltpu.roll(d, lanes - 1, 1))
            ahead = recip(d + beyond)
            wz[p + 1, pl.ds(r, n)] = jnp.where(lane == lanes - 1, 0.0, ahead)
            behind = jnp.where(lane == 0, recip(d), pltpu.roll(ahead, 1, 1))
            diag = wx[p + 2, pl.ds(r, n)] + wx[p + 1, pl.ds(r, n)]
            diag = diag + up + wy[p + 1, pl.ds(r - 1, n)] + ahead + behind
            b = recip(diag)
            inv[p + 1, pl.ds(r, n)] = b
            if rim or TOP <= r < end:
                q = keep_y(r, b * src[p + 1, pl.ds(r, n)])
                if keep is not None:
                    q = jnp.where(keep, q, 0.0)
                q0[p + 2, pl.ds(r, n)] = q

    def rim_field(p):
        for r, n in (spans[0], spans[-1]):
            q0[p + 2, pl.ds(r, n)] = keep_y(r, inv[p + 1, pl.ds(r, n)] * src[p + 1, pl.ds(r, n)])

    def coupled(v, shift, p, r, n):
        mid = v[p + shift, pl.ds(r, n)]
        total = wx[p + 2, pl.ds(r, n)] * v[p + shift + 1, pl.ds(r, n)]
        total = total + wx[p + 1, pl.ds(r, n)] * v[p + shift - 1, pl.ds(r, n)]
        total = total + wy[p + 1, pl.ds(r, n)] * v[p + shift, pl.ds(r + 1, n)]
        total = total + wy[p + 1, pl.ds(r - 1, n)] * v[p + shift, pl.ds(r - 1, n)]
        w = wz[p + 1, pl.ds(r, n)]
        total = total + w * pltpu.roll(mid, lanes - 1, 1)
        return mid, total + pltpu.roll(w * mid, 1, 1)

    def first_apply(p, sums, keep=None, own=True):
        g0, d0, ss = sums
        for r, n in spans if own else mids:
            mid, total = coupled(q0, 2, p, r, n)
            s = src[p + 1, pl.ds(r, n)]
            t = s - total
            q = keep_y(r, inv[p + 1, pl.ds(r, n)] * t)
            if keep is not None:
                q = jnp.where(keep, q, 0.0)
            q1[p + 1, pl.ds(r, n)] = q
            if own and TOP <= r < end:
                t1_out[p, pl.ds(r - TOP, n)] = t
                g0 = g0 + fold(s * mid)
                d0 = d0 + fold(t * mid)
                ss = ss + fold(t * q)
        return g0, d0, ss

    def second_apply(p, h):
        for r, n in mids:
            mid, total = coupled(q1, 1, p, r, n)
            t = t1_out[p, pl.ds(r - TOP, n)] - total
            t2_out[p, pl.ds(r - TOP, n)] = t
            h = h + fold(t * mid)
        return h

    def over(start, step, count, f, carry=None):
        def go(k, c):
            return f(start + step * k, c)
        return lax.fori_loop(0, count, go, carry)

    def plain(f):
        def g(p, c):
            f(p)
            return c
        return g

    zero = jnp.zeros((8, 128), F32)
    tell(0)
    load_d.wait()
    over(0, 1, last, plain(lambda p: faces_x(p, mids)), 0)
    load_s.wait()
    arrive(rim_d)

    @pl.when(j == 0)
    def _():
        den[2 : depth + 2, TOP - 8 : TOP] = jnp.zeros((depth, 8, lanes), F32)

    @pl.when(j == ny - 1)
    def _():
        den[2 : depth + 2, end : end + 8] = jnp.zeros((depth, 8, lanes), F32)

    over(0, 1, last, plain(lambda p: faces_x(p, (spans[0], spans[-1]))), 0)
    over(1, last - 2, 2, plain(lambda p: inverse(p, rim=False)), 0)
    for copy in field:
        copy.start()
    heard(0)
    tell(1)
    over(2, 1, depth - 4, plain(lambda p: inverse(p, rim=False)), 0)
    arrive(rim_s)
    over(1, 1, depth - 2, plain(rim_field), 0)
    sums = over(2, 1, depth - 4, first_apply, (zero, zero, zero))

    heard(1)
    tell(2)
    arrive(face_d)
    arrive(corner_d)
    for edge, first, there in ((0, i == 0, 0), (nx - 1, i == nx - 1, depth + 2)):
        @pl.when(first)
        def _():
            near = there + 1 if edge == 0 else there
            den[near, TOP - 8 : end + 8] = jnp.zeros((width + 16, lanes), F32)
    for bound, first, rows in ((0, j == 0, TOP - 8), (ny - 1, j == ny - 1, end)):
        @pl.when(first)
        def _():
            den[0:2, rows : rows + 8] = jnp.zeros((2, 8, lanes), F32)
            den[depth + 2 : depth + 4, rows : rows + 8] = jnp.zeros((2, 8, lanes), F32)

    over(-1, depth, 2, plain(faces_x), 0)
    arrive(corner_s)
    over(0, last, 2, plain(inverse), 0)
    sums = over(1, last - 2, 2, first_apply, sums)

    heard(2)
    tell(3)
    arrive(face_s)
    arrive(second_d)
    over(-2, depth + 2, 2, plain(faces_x), 0)

    def outer(p):
        return jnp.logical_or(jnp.logical_and(p < 0, i > 0), jnp.logical_and(p > 0, i < nx - 1))

    over(-1, depth + 1, 2, plain(lambda p: inverse(p, keep=outer(p))), 0)
    g0, d0, ss = over(0, last, 2, first_apply, sums)
    h = over(1, 1, depth - 2, second_apply, zero)

    arrive(field)
    over(-1, depth + 1, 2, plain(lambda p: first_apply(p, (None,) * 3, keep=outer(p), own=False)), 0)
    h = over(0, last, 2, second_apply, h)

    group = lax.broadcasted_iota(jnp.int32, (1, 128), 1) // 32
    row = jnp.zeros((1, 128), F32)
    for k, part in enumerate((g0, d0, ss, h)):
        v = jnp.sum(part, axis=0, keepdims=True)
        v = v + pltpu.roll(v, 64, 1)
        v = v + pltpu.roll(v, 32, 1)
        row = jnp.where(group == k, v, row)

    def spread(k, value, peers, got):
        msg[k] = value
        for s, peer in enumerate(peers):
            pltpu.make_async_remote_copy(
                src_ref=msg.at[k], dst_ref=got.at[s], send_sem=sum_send.at[k], recv_sem=sum_recv.at[k],
                device_id=peer, device_id_type=MESH).start()

    def gathered(k, value, got):
        pltpu.make_async_copy(got, got, sum_recv.at[k]).wait()
        for s in range(got.shape[0]):
            value = value + got[s]
        return value

    spread(0, row, row_peers, got_y)

    def scales(p):
        for r, n in mids:
            rows = pl.ds(r - TOP, n)
            half = 0.5 * inv[p + 1, pl.ds(r, n)]
            scale = half * lax.rsqrt(half)
            scale_out[p, rows] = scale
            t0_out[p, rows] = scale * src[p + 1, pl.ds(r, n)]
            t1_out[p, rows] = scale * t1_out[p, rows]
            t2_out[p, rows] = scale * t2_out[p, rows]

    over(0, 1, depth, plain(scales), 0)
    row = gathered(0, row, got_y)
    heard(3)
    spread(1, row, col_peers, got_x)
    for copy in copies:
        copy.wait_send()
    row = gathered(1, row, got_x)
    pltpu.make_async_copy(got_y, got_y, sum_send.at[0]).wait()
    pltpu.make_async_copy(got_x, got_x, sum_send.at[1]).wait()

    def total(k):
        return jnp.broadcast_to(jnp.sum(jnp.where(group == k, row, 0.0), axis=1, keepdims=True), (1, 128))

    g0, d0, ss, h = (total(k) for k in range(4))
    alpha0 = g0 / d0
    gamma1 = g0 - 2.0 * alpha0 * d0 + alpha0 * alpha0 * ss
    delta1 = d0 - 2.0 * alpha0 * ss + alpha0 * alpha0 * h
    beta1 = gamma1 / g0
    alpha1 = gamma1 / (delta1 - beta1 * gamma1 / alpha0)
    coef_out[0:1] = alpha0 + alpha1 * (1.0 + beta1)
    coef_out[1:2] = alpha0 * alpha1


def combine(t0, t1, t2, scale, coef, pressure, residual, held_p, held_r, sem):
    a, b = coef[0:1, 0:1], coef[1:2, 0:1]
    copies = []
    for p in range(t0.shape[0]):
        u0, u1 = t0[p], t1[p]
        held_p[p] = scale[p] * (a * u0 - b * u1)
        held_r[p] = u0 - a * u1 + b * t2[p]
        for k, (held, out) in enumerate(((held_p, pressure), (held_r, residual))):
            copies.append(pltpu.make_async_copy(held.at[p], out.at[p], sem.at[k, p]))
            copies[-1].start()
    for copy in copies:
        copy.wait()


def solution(mesh):
    sizes = (mesh.shape["gx"], mesh.shape["gy"])

    def shards(source, density):
        depth, width, lanes = source.shape
        shape = jax.ShapeDtypeStruct(source.shape, F32)

        def planes(n):
            return pltpu.VMEM((n, TOP + width + 16, lanes), F32)

        vmem = pl.BlockSpec(memory_space=pltpu.VMEM)
        hbm = pl.BlockSpec(memory_space=pltpu.HBM)
        t0, t1, t2, scale, coef = pl.pallas_call(
            functools.partial(kernel, sizes),
            out_shape=(shape,) * 4 + (jax.ShapeDtypeStruct((2, 128), F32),),
            in_specs=[hbm] * 2,
            out_specs=(vmem,) * 5,
            scratch_shapes=[
                planes(depth + 4), planes(depth + 2), planes(depth + 4), planes(depth + 2),
                planes(depth + 2), planes(depth + 3), planes(depth + 2), planes(depth + 2),
                pltpu.VMEM((2, 1, 128), F32),
                pltpu.VMEM((sizes[1] - 1, 1, 128), F32),
                pltpu.VMEM((sizes[0] - 1, 1, 128), F32),
                pltpu.SemaphoreType.DMA((2,)),
                pltpu.SemaphoreType.DMA((20,)),
                pltpu.SemaphoreType.DMA((20,)),
                pltpu.SemaphoreType.DMA((2,)),
                pltpu.SemaphoreType.DMA((2,)),
                pltpu.SemaphoreType.REGULAR((4,)),
            ],
            compiler_params=pltpu.CompilerParams(
                collective_id=1, has_side_effects=True, vmem_limit_bytes=36 * 1024 * 1024),
        )(pltpu.with_memory_space_constraint(source, pltpu.HBM), pltpu.with_memory_space_constraint(density, pltpu.HBM))
        pressure, residual = pl.pallas_call(
            combine,
            out_shape=(shape, shape),
            in_specs=[vmem] * 5,
            out_specs=(hbm, hbm),
            scratch_shapes=[
                pltpu.VMEM(source.shape, F32), pltpu.VMEM(source.shape, F32), pltpu.SemaphoreType.DMA((2, depth))],
            compiler_params=pltpu.CompilerParams(vmem_limit_bytes=16 * 1024 * 1024),
        )(t0, t1, t2, scale, coef)
        return pressure, residual

    spec = P("gx", "gy", None)
    return jax.shard_map(shards, mesh=mesh, in_specs=(spec, spec), out_specs=(spec, spec), check_vma=False)
```

```python
import functools

import jax
import jax.numpy as jnp
from jax import lax
from jax.experimental import pallas as pl
from jax.experimental.pallas import tpu as pltpu
from jax.sharding import PartitionSpec as P

MESH = pl.DeviceIdType.MESH
F32 = jnp.float32
TOP = 16


def recip(x):
    r = pl.reciprocal(x, approx=True)
    return r * (2.0 - x * r)


def fold(v):
    rows, lanes = v.shape
    out = None
    for r in range(0, rows, 8):
        for c in range(0, lanes, 128):
            piece = v[r : r + 8, c : c + 128]
            out = piece if out is None else out + piece
    return out


def kernel(sizes, source, density, t0_out, t1_out, t2_out, scale_out, coef_out,
           den, src, q0, q1, inv, wx, wy, wz, msg, got_y, got_x,
           local_sem, send_sem, recv_sem, sum_send, sum_recv, known):
    nx, ny = sizes
    depth, width, lanes = t1_out.shape
    end = TOP + width
    last = depth - 1
    i, j = lax.axis_index("gx"), lax.axis_index("gy")
    right, left = (i + 1, i < nx - 1, i > 0), (i - 1, i > 0, i < nx - 1)
    above, below = (j + 1, j < ny - 1, j > 0), (j - 1, j > 0, j < ny - 1)

    def beside(a, b):
        both = jnp.logical_and
        return ((a[0], b[0]), both(a[1], b[1]), both(a[2], b[2]))

    sides = [((right[0], j), right[1], right[2]), ((left[0], j), left[1], left[2])]
    side = int(ny**0.5)
    chips = nx // 2
    core = lax.rem(i, 2)

    def far(k, n):
        return min(k, n - k)

    offsets = [(b, a, c) for b in range(side) for a in range(side) for c in range(2)][1:]
    offsets.sort(key=lambda o: -far(o[0], side) - far(o[1], side))
    row_peers = [
        (i + c * (1 - 2 * core), lax.rem(j // side + b, side) * side + lax.rem(lax.rem(j, side) + a, side))
        for b, a, c in offsets
    ]
    col_peers = [
        (lax.rem(i + 2 * k, nx), j) for k in sorted(range(1, chips), key=lambda k: -far(k, chips))
    ]
    corners = [beside(a, b) for a in (right, left) for b in (above, below)]

    body, low, high = pl.ds(TOP, width), pl.ds(TOP - 8, 8), pl.ds(end, 8)
    load_d = pltpu.make_async_copy(density, den.at[pl.ds(2, depth), body], local_sem.at[0])
    load_s = pltpu.make_async_copy(source, src.at[pl.ds(1, depth), body], local_sem.at[1])
    load_d.start()
    load_s.start()

    barrier = pltpu.get_barrier_semaphore()
    for peer in row_peers + [(lax.rem(i + 2, nx), j), (lax.rem(i + nx - 2, nx), j)]:
        pl.semaphore_signal(barrier, inc=1, device_id=peer, device_id_type=MESH)
    across = i + 2 * core - 1
    inside = jnp.logical_and(across >= 0, across < nx)
    for row, there in ((j, True), (j + 1, j < ny - 1), (j - 1, j > 0)):
        @pl.when(jnp.logical_and(inside, there))
        def _():
            pl.semaphore_signal(barrier, inc=1, device_id=(across, row), device_id_type=MESH)
    beside_y = (j > 0).astype(jnp.int32) + (j < ny - 1).astype(jnp.int32)
    pl.semaphore_wait(barrier, len(row_peers) + 2 + inside.astype(jnp.int32) * (1 + beside_y))

    rounds = (chips - 1).bit_length() - 1

    def tell(k):
        if k < rounds:
            for step in (2 ** (k + 1), nx - 2 ** (k + 1)):
                pl.semaphore_signal(
                    known.at[k], inc=1, device_id=(lax.rem(i + step, nx), j), device_id_type=MESH)

    def heard(k):
        if k < rounds:
            pl.semaphore_wait(known.at[k], 2)

    copies = []

    def send(what, where, peer):
        k = len(copies)
        who, there, opposite = peer
        copies.append((pltpu.make_async_remote_copy(
            src_ref=what, dst_ref=where, send_sem=send_sem.at[k], recv_sem=recv_sem.at[k],
            device_id=who, device_id_type=MESH), there, opposite))
        return copies[-1]

    def begin(group):
        for copy, there, _ in group:
            pl.when(there)(copy.start)

    top_rows, first_rows = pl.ds(width - 8, 8), pl.ds(0, 8)
    own_d, own_s = pl.ds(2, depth), pl.ds(1, depth)
    rim_d = [
        send(density.at[:, top_rows], den.at[own_d, low], ((i, above[0]), above[1], above[2])),
        send(density.at[:, first_rows], den.at[own_d, high], ((i, below[0]), below[1], below[2])),
    ]
    face_d = [
        send(density.at[last], den.at[1, body], sides[0]),
        send(density.at[0], den.at[depth + 2, body], sides[1]),
    ]
    rim_s = [
        send(source.at[:, top_rows], src.at[own_s, low], ((i, above[0]), above[1], above[2])),
        send(source.at[:, first_rows], src.at[own_s, high], ((i, below[0]), below[1], below[2])),
    ]
    corner_d, corner_s = [], []
    for a in (right, left):
        plane, there = (last - 1, 0) if a is right else (0, depth + 2)
        face, face_there = (last, 0) if a is right else (0, depth + 1)
        for b, rows, place in ((above, top_rows, low), (below, first_rows, high)):
            corner_d.append(send(density.at[pl.ds(plane, 2), rows], den.at[pl.ds(there, 2), place], beside(a, b)))
            corner_s.append(send(source.at[face, rows], src.at[face_there, place], beside(a, b)))
    face_s = [
        send(source.at[last], src.at[0, body], sides[0]),
        send(source.at[0], src.at[depth + 1, body], sides[1]),
    ]
    second_d = [
        send(density.at[last - 1], den.at[0, body], sides[0]),
        send(density.at[1], den.at[depth + 3, body], sides[1]),
    ]
    begin(copies)
    field = [
        send(q0.at[last - 1 + 2, body], q0.at[0, body], sides[0]),
        send(q0.at[1 + 2, body], q0.at[depth + 3, body], sides[1]),
    ]

    def arrive(group):
        for copy, _, opposite in group:
            pl.when(opposite)(copy.wait_recv)

    mids = [(r, 16) for r in range(TOP, end, 16)]
    spans = [(TOP - 8, 8)] + mids + [(end, 8)]

    def keep_y(r, v):
        if r < TOP:
            return jnp.where(j > 0, v, 0.0)
        if r >= end:
            return jnp.where(j < ny - 1, v, 0.0)
        return v

    def faces_x(p, rows=spans):
        for r, n in rows:
            wx[p + 2, pl.ds(r, n)] = recip(den[p + 2, pl.ds(r, n)] + den[p + 3, pl.ds(r, n)])

    def inverse(p, keep=None, rim=True):
        for r, n in spans:
            d = den[p + 2, pl.ds(r, n)]
            lane = lax.broadcasted_iota(jnp.int32, (n, lanes), 1)
            up = recip(d + den[p + 2, pl.ds(r + 1, n)])
            wy[p + 1, pl.ds(r, n)] = up
            beyond = jnp.where(lane == lanes - 1, 0.0, pltpu.roll(d, lanes - 1, 1))
            ahead = recip(d + beyond)
            wz[p + 1, pl.ds(r, n)] = jnp.where(lane == lanes - 1, 0.0, ahead)
            behind = jnp.where(lane == 0, recip(d), pltpu.roll(ahead, 1, 1))
            diag = wx[p + 2, pl.ds(r, n)] + wx[p + 1, pl.ds(r, n)]
            diag = diag + up + wy[p + 1, pl.ds(r - 1, n)] + ahead + behind
            b = recip(diag)
            inv[p + 1, pl.ds(r, n)] = b
            if rim or TOP <= r < end:
                q = keep_y(r, b * src[p + 1, pl.ds(r, n)])
                if keep is not None:
                    q = jnp.where(keep, q, 0.0)
                q0[p + 2, pl.ds(r, n)] = q

    def rim_field(p):
        for r, n in (spans[0], spans[-1]):
            q0[p + 2, pl.ds(r, n)] = keep_y(r, inv[p + 1, pl.ds(r, n)] * src[p + 1, pl.ds(r, n)])

    def coupled(v, shift, p, r, n):
        mid = v[p + shift, pl.ds(r, n)]
        total = wx[p + 2, pl.ds(r, n)] * v[p + shift + 1, pl.ds(r, n)]
        total = total + wx[p + 1, pl.ds(r, n)] * v[p + shift - 1, pl.ds(r, n)]
        total = total + wy[p + 1, pl.ds(r, n)] * v[p + shift, pl.ds(r + 1, n)]
        total = total + wy[p + 1, pl.ds(r - 1, n)] * v[p + shift, pl.ds(r - 1, n)]
        w = wz[p + 1, pl.ds(r, n)]
        total = total + w * pltpu.roll(mid, lanes - 1, 1)
        return mid, total + pltpu.roll(w * mid, 1, 1)

    def first_apply(p, sums, keep=None, own=True):
        g0, d0, ss = sums
        for r, n in spans if own else mids:
            mid, total = coupled(q0, 2, p, r, n)
            s = src[p + 1, pl.ds(r, n)]
            t = s - total
            q = keep_y(r, inv[p + 1, pl.ds(r, n)] * t)
            if keep is not None:
                q = jnp.where(keep, q, 0.0)
            q1[p + 1, pl.ds(r, n)] = q
            if own and TOP <= r < end:
                t1_out[p, pl.ds(r - TOP, n)] = t
                g0 = g0 + fold(s * mid)
                d0 = d0 + fold(t * mid)
                ss = ss + fold(t * q)
        return g0, d0, ss

    def second_apply(p, h):
        for r, n in mids:
            mid, total = coupled(q1, 1, p, r, n)
            t = t1_out[p, pl.ds(r - TOP, n)] - total
            t2_out[p, pl.ds(r - TOP, n)] = t
            h = h + fold(t * mid)
        return h

    def over(start, step, count, f, carry=None):
        def go(k, c):
            return f(start + step * k, c)
        return lax.fori_loop(0, count, go, carry)

    def plain(f):
        def g(p, c):
            f(p)
            return c
        return g

    zero = jnp.zeros((8, 128), F32)
    tell(0)
    load_d.wait()
    over(0, 1, last, plain(lambda p: faces_x(p, mids)), 0)
    load_s.wait()
    heard(0)
    tell(1)
    arrive(rim_d)

    @pl.when(j == 0)
    def _():
        den[2 : depth + 2, TOP - 8 : TOP] = jnp.zeros((depth, 8, lanes), F32)

    @pl.when(j == ny - 1)
    def _():
        den[2 : depth + 2, end : end + 8] = jnp.zeros((depth, 8, lanes), F32)

    over(0, 1, last, plain(lambda p: faces_x(p, (spans[0], spans[-1]))), 0)
    over(1, last - 2, 2, plain(lambda p: inverse(p, rim=False)), 0)
    begin(field)
    over(2, 1, depth - 4, plain(lambda p: inverse(p, rim=False)), 0)
    heard(1)
    tell(2)
    arrive(rim_s)
    over(1, 1, depth - 2, plain(rim_field), 0)
    sums = over(2, 1, depth - 4, first_apply, (zero, zero, zero))

    arrive(face_d)
    arrive(corner_d)
    for edge, first, there in ((0, i == 0, 0), (nx - 1, i == nx - 1, depth + 2)):
        @pl.when(first)
        def _():
            near = there + 1 if edge == 0 else there
            den[near, TOP - 8 : end + 8] = jnp.zeros((width + 16, lanes), F32)
    for bound, first, rows in ((0, j == 0, TOP - 8), (ny - 1, j == ny - 1, end)):
        @pl.when(first)
        def _():
            den[0:2, rows : rows + 8] = jnp.zeros((2, 8, lanes), F32)
            den[depth + 2 : depth + 4, rows : rows + 8] = jnp.zeros((2, 8, lanes), F32)

    over(-1, depth, 2, plain(faces_x), 0)
    arrive(corner_s)
    over(0, last, 2, plain(inverse), 0)
    sums = over(1, last - 2, 2, first_apply, sums)

    arrive(face_s)
    arrive(second_d)
    over(-2, depth + 2, 2, plain(faces_x), 0)

    def outer(p):
        return jnp.logical_or(jnp.logical_and(p < 0, i > 0), jnp.logical_and(p > 0, i < nx - 1))

    over(-1, depth + 1, 2, plain(lambda p: inverse(p, keep=outer(p))), 0)
    g0, d0, ss = over(0, last, 2, first_apply, sums)
    h = over(1, 1, depth - 2, second_apply, zero)

    arrive(field)
    over(-1, depth + 1, 2, plain(lambda p: first_apply(p, (None,) * 3, keep=outer(p), own=False)), 0)
    h = over(0, last, 2, second_apply, h)

    group = lax.broadcasted_iota(jnp.int32, (1, 128), 1) // 32
    row = jnp.zeros((1, 128), F32)
    for k, part in enumerate((g0, d0, ss, h)):
        v = jnp.sum(part, axis=0, keepdims=True)
        v = v + pltpu.roll(v, 64, 1)
        v = v + pltpu.roll(v, 32, 1)
        row = jnp.where(group == k, v, row)

    def spread(k, value, peers, got):
        msg[k] = value
        for s, peer in enumerate(peers):
            pltpu.make_async_remote_copy(
                src_ref=msg.at[k], dst_ref=got.at[s], send_sem=sum_send.at[k], recv_sem=sum_recv.at[k],
                device_id=peer, device_id_type=MESH).start()

    def gathered(k, value, got):
        pltpu.make_async_copy(got, got, sum_recv.at[k]).wait()
        for s in range(got.shape[0]):
            value = value + got[s]
        return value

    spread(0, row, row_peers, got_y)

    def scales(p):
        for r, n in mids:
            rows = pl.ds(r - TOP, n)
            half = 0.5 * inv[p + 1, pl.ds(r, n)]
            scale = half * lax.rsqrt(half)
            scale_out[p, rows] = scale
            t0_out[p, rows] = scale * src[p + 1, pl.ds(r, n)]
            t1_out[p, rows] = scale * t1_out[p, rows]
            t2_out[p, rows] = scale * t2_out[p, rows]

    over(0, 1, depth, plain(scales), 0)
    row = gathered(0, row, got_y)
    heard(2)
    spread(1, row, col_peers, got_x)
    for copy, there, _ in copies:
        pl.when(there)(copy.wait_send)
    row = gathered(1, row, got_x)
    pltpu.make_async_copy(got_y, got_y, sum_send.at[0]).wait()
    pltpu.make_async_copy(got_x, got_x, sum_send.at[1]).wait()

    def total(k):
        return jnp.broadcast_to(jnp.sum(jnp.where(group == k, row, 0.0), axis=1, keepdims=True), (1, 128))

    g0, d0, ss, h = (total(k) for k in range(4))
    alpha0 = g0 / d0
    gamma1 = g0 - 2.0 * alpha0 * d0 + alpha0 * alpha0 * ss
    delta1 = d0 - 2.0 * alpha0 * ss + alpha0 * alpha0 * h
    beta1 = gamma1 / g0
    alpha1 = gamma1 / (delta1 - beta1 * gamma1 / alpha0)
    coef_out[0:1] = alpha0 + alpha1 * (1.0 + beta1)
    coef_out[1:2] = alpha0 * alpha1


def combine(t0, t1, t2, scale, coef, pressure, residual, held_p, held_r, sem):
    a, b = coef[0:1, 0:1], coef[1:2, 0:1]
    copies = []
    for p in range(t0.shape[0]):
        u0, u1 = t0[p], t1[p]
        held_p[p] = scale[p] * (a * u0 - b * u1)
        held_r[p] = u0 - a * u1 + b * t2[p]
        for k, (held, out) in enumerate(((held_p, pressure), (held_r, residual))):
            copies.append(pltpu.make_async_copy(held.at[p], out.at[p], sem.at[k, p]))
            copies[-1].start()
    for copy in copies:
        copy.wait()


def solution(mesh):
    sizes = (mesh.shape["gx"], mesh.shape["gy"])

    def shards(source, density):
        depth, width, lanes = source.shape
        shape = jax.ShapeDtypeStruct(source.shape, F32)

        def planes(n):
            return pltpu.VMEM((n, TOP + width + 16, lanes), F32)

        vmem = pl.BlockSpec(memory_space=pltpu.VMEM)
        hbm = pl.BlockSpec(memory_space=pltpu.HBM)
        t0, t1, t2, scale, coef = pl.pallas_call(
            functools.partial(kernel, sizes),
            out_shape=(shape,) * 4 + (jax.ShapeDtypeStruct((2, 128), F32),),
            in_specs=[hbm] * 2,
            out_specs=(vmem,) * 5,
            scratch_shapes=[
                planes(depth + 4), planes(depth + 2), planes(depth + 4), planes(depth + 2),
                planes(depth + 2), planes(depth + 3), planes(depth + 2), planes(depth + 2),
                pltpu.VMEM((2, 1, 128), F32),
                pltpu.VMEM((2 * sizes[1] - 1, 1, 128), F32),
                pltpu.VMEM((sizes[0] // 2 - 1, 1, 128), F32),
                pltpu.SemaphoreType.DMA((2,)),
                pltpu.SemaphoreType.DMA((20,)),
                pltpu.SemaphoreType.DMA((20,)),
                pltpu.SemaphoreType.DMA((2,)),
                pltpu.SemaphoreType.DMA((2,)),
                pltpu.SemaphoreType.REGULAR((3,)),
            ],
            compiler_params=pltpu.CompilerParams(
                collective_id=1, has_side_effects=True, vmem_limit_bytes=36 * 1024 * 1024),
        )(pltpu.with_memory_space_constraint(source, pltpu.HBM), pltpu.with_memory_space_constraint(density, pltpu.HBM))
        pressure, residual = pl.pallas_call(
            combine,
            out_shape=(shape, shape),
            in_specs=[vmem] * 5,
            out_specs=(hbm, hbm),
            scratch_shapes=[
                pltpu.VMEM(source.shape, F32), pltpu.VMEM(source.shape, F32), pltpu.SemaphoreType.DMA((2, depth))],
            compiler_params=pltpu.CompilerParams(vmem_limit_bytes=16 * 1024 * 1024),
        )(t0, t1, t2, scale, coef)
        return pressure, residual

    spec = P("gx", "gy", None)
    return jax.shard_map(shards, mesh=mesh, in_specs=(spec, spec), out_specs=(spec, spec), check_vma=False)
```

```python
import functools

import jax
import jax.numpy as jnp
from jax import lax
from jax.experimental import pallas as pl
from jax.experimental.pallas import tpu as pltpu
from jax.sharding import PartitionSpec as P

MESH = pl.DeviceIdType.MESH
F32 = jnp.float32
TOP = 16


def recip(x):
    r = pl.reciprocal(x, approx=True)
    return r * (2.0 - x * r)


def fold(v):
    rows, lanes = v.shape
    out = None
    for r in range(0, rows, 8):
        for c in range(0, lanes, 128):
            piece = v[r : r + 8, c : c + 128]
            out = piece if out is None else out + piece
    return out


def kernel(sizes, source, density, t0_out, t1_out, t2_out, scale_out, coef_out,
           den, src, q0, q1, inv, wx, wy, wz, msg, got_y, got_x,
           local_sem, send_sem, recv_sem, sum_send, sum_recv, known):
    nx, ny = sizes
    depth, width, lanes = t1_out.shape
    end = TOP + width
    last = depth - 1
    i, j = lax.axis_index("gx"), lax.axis_index("gy")
    right, left = (i + 1, i < nx - 1, i > 0), (i - 1, i > 0, i < nx - 1)
    above, below = (j + 1, j < ny - 1, j > 0), (j - 1, j > 0, j < ny - 1)

    def beside(a, b):
        both = jnp.logical_and
        return ((a[0], b[0]), both(a[1], b[1]), both(a[2], b[2]))

    sides = [((right[0], j), right[1], right[2]), ((left[0], j), left[1], left[2])]
    side = int(ny**0.5)
    chips = nx // 2
    core = lax.rem(i, 2)

    def far(k, n):
        return min(k, n - k)

    offsets = [(b, a, c) for b in range(side) for a in range(side) for c in range(2)][1:]
    offsets.sort(key=lambda o: -far(o[0], side) - far(o[1], side))
    row_peers = [
        (i + c * (1 - 2 * core), lax.rem(j // side + b, side) * side + lax.rem(lax.rem(j, side) + a, side))
        for b, a, c in offsets
    ]
    col_peers = [
        (lax.rem(i + 2 * k, nx), j) for k in sorted(range(1, chips), key=lambda k: -far(k, chips))
    ]
    corners = [beside(a, b) for a in (right, left) for b in (above, below)]

    body, low, high = pl.ds(TOP, width), pl.ds(TOP - 8, 8), pl.ds(end, 8)
    load_d = pltpu.make_async_copy(density, den.at[pl.ds(2, depth), body], local_sem.at[0])
    load_s = pltpu.make_async_copy(source, src.at[pl.ds(1, depth), body], local_sem.at[1])
    load_d.start()
    load_s.start()

    barrier = pltpu.get_barrier_semaphore()
    across = i + 2 * core - 1
    inside = jnp.logical_and(across >= 0, across < nx)
    for row, there in ((j, True), (j + 1, j < ny - 1), (j - 1, j > 0)):
        @pl.when(jnp.logical_and(inside, there))
        def _():
            pl.semaphore_signal(barrier, inc=1, device_id=(across, row), device_id_type=MESH)
    for peer in [(lax.rem(i + 2, nx), j), (lax.rem(i + nx - 2, nx), j)] + row_peers[::-1]:
        pl.semaphore_signal(barrier, inc=1, device_id=peer, device_id_type=MESH)
    beside_y = (j > 0).astype(jnp.int32) + (j < ny - 1).astype(jnp.int32)

    rounds = (chips - 1).bit_length() - 1

    def tell(k):
        if k < rounds:
            for step in (2 ** (k + 1), nx - 2 ** (k + 1)):
                pl.semaphore_signal(
                    known.at[k], inc=1, device_id=(lax.rem(i + step, nx), j), device_id_type=MESH)

    def heard(k):
        if k < rounds:
            pl.semaphore_wait(known.at[k], 2)

    def arrive(group):
        for copy, _, opposite in group:
            pl.when(opposite)(copy.wait_recv)

    mids = [(r, 16) for r in range(TOP, end, 16)]
    spans = [(TOP - 8, 8)] + mids + [(end, 8)]

    def keep_y(r, v):
        if r < TOP:
            return jnp.where(j > 0, v, 0.0)
        if r >= end:
            return jnp.where(j < ny - 1, v, 0.0)
        return v

    def faces_x(p, rows=spans):
        for r, n in rows:
            wx[p + 2, pl.ds(r, n)] = recip(den[p + 2, pl.ds(r, n)] + den[p + 3, pl.ds(r, n)])

    def faces_y(p, rows=spans):
        for r, n in rows:
            wy[p + 1, pl.ds(r, n)] = recip(den[p + 2, pl.ds(r, n)] + den[p + 2, pl.ds(r + 1, n)])

    def inverse(p, rows=spans, keep=None, rim=True):
        for r, n in rows:
            d = den[p + 2, pl.ds(r, n)]
            lane = lax.broadcasted_iota(jnp.int32, (n, lanes), 1)
            beyond = jnp.where(lane == lanes - 1, 0.0, pltpu.roll(d, lanes - 1, 1))
            ahead = recip(d + beyond)
            wz[p + 1, pl.ds(r, n)] = jnp.where(lane == lanes - 1, 0.0, ahead)
            behind = jnp.where(lane == 0, recip(d), pltpu.roll(ahead, 1, 1))
            diag = wx[p + 2, pl.ds(r, n)] + wx[p + 1, pl.ds(r, n)]
            diag = diag + wy[p + 1, pl.ds(r, n)] + wy[p + 1, pl.ds(r - 1, n)] + ahead + behind
            b = recip(diag)
            inv[p + 1, pl.ds(r, n)] = b
            if rim or TOP <= r < end:
                q = keep_y(r, b * src[p + 1, pl.ds(r, n)])
                if keep is not None:
                    q = jnp.where(keep, q, 0.0)
                q0[p + 2, pl.ds(r, n)] = q

    def whole(p, keep=None):
        faces_y(p)
        inverse(p, spans, keep)

    def rim_field(p):
        for r, n in (spans[0], spans[-1]):
            q0[p + 2, pl.ds(r, n)] = keep_y(r, inv[p + 1, pl.ds(r, n)] * src[p + 1, pl.ds(r, n)])

    def coupled(v, shift, p, r, n):
        mid = v[p + shift, pl.ds(r, n)]
        total = wx[p + 2, pl.ds(r, n)] * v[p + shift + 1, pl.ds(r, n)]
        total = total + wx[p + 1, pl.ds(r, n)] * v[p + shift - 1, pl.ds(r, n)]
        total = total + wy[p + 1, pl.ds(r, n)] * v[p + shift, pl.ds(r + 1, n)]
        total = total + wy[p + 1, pl.ds(r - 1, n)] * v[p + shift, pl.ds(r - 1, n)]
        w = wz[p + 1, pl.ds(r, n)]
        total = total + w * pltpu.roll(mid, lanes - 1, 1)
        return mid, total + pltpu.roll(w * mid, 1, 1)

    def first_apply(p, sums, rows=spans, keep=None, own=True):
        g0, d0, ss = sums
        for r, n in rows:
            mid, total = coupled(q0, 2, p, r, n)
            s = src[p + 1, pl.ds(r, n)]
            t = s - total
            q = keep_y(r, inv[p + 1, pl.ds(r, n)] * t)
            if keep is not None:
                q = jnp.where(keep, q, 0.0)
            q1[p + 1, pl.ds(r, n)] = q
            if own and TOP <= r < end:
                t1_out[p, pl.ds(r - TOP, n)] = t
                g0 = g0 + fold(s * mid)
                d0 = d0 + fold(t * mid)
                ss = ss + fold(t * q)
        return g0, d0, ss

    def second_apply(p, h):
        for r, n in mids:
            mid, total = coupled(q1, 1, p, r, n)
            t = t1_out[p, pl.ds(r - TOP, n)] - total
            t2_out[p, pl.ds(r - TOP, n)] = t
            h = h + fold(t * mid)
        return h

    def over(start, step, count, f, carry=None):
        def go(k, c):
            return f(start + step * k, c)
        return lax.fori_loop(0, count, go, carry)

    def plain(f):
        def g(p, c):
            f(p)
            return c
        return g

    copies = []

    def send(what, where, peer):
        k = len(copies)
        who, there, opposite = peer
        copies.append((pltpu.make_async_remote_copy(
            src_ref=what, dst_ref=where, send_sem=send_sem.at[k], recv_sem=recv_sem.at[k],
            device_id=who, device_id_type=MESH), there, opposite))
        return copies[-1]

    def begin(group):
        for copy, there, _ in group:
            pl.when(there)(copy.start)

    own_d, own_s = pl.ds(2, depth), pl.ds(1, depth)

    def ends(n):
        return ((above, pl.ds(width - n, n), pl.ds(TOP - n, n)), (below, pl.ds(0, n), pl.ds(end, n)))

    rim_d = [send(density.at[:, rows], den.at[own_d, place], ((i, b[0]), b[1], b[2])) for b, rows, place in ends(3)]
    face_d = [
        send(density.at[last], den.at[1, body], sides[0]),
        send(density.at[0], den.at[depth + 2, body], sides[1]),
    ]
    rim_s = [send(source.at[:, rows], src.at[own_s, place], ((i, b[0]), b[1], b[2])) for b, rows, place in ends(2)]
    corner_d, corner_s = [], []
    for a in (right, left):
        plane, there = (last - 1, 0) if a is right else (0, depth + 2)
        face, face_there = (last, 0) if a is right else (0, depth + 1)
        for b, rows, place in ends(2):
            corner_d.append(send(density.at[pl.ds(plane, 2), rows], den.at[pl.ds(there, 2), place], beside(a, b)))
        for b, rows, place in ends(1):
            corner_s.append(send(source.at[face, rows], src.at[face_there, place], beside(a, b)))
    face_s = [
        send(source.at[last], src.at[0, body], sides[0]),
        send(source.at[0], src.at[depth + 1, body], sides[1]),
    ]
    second_d = [
        send(density.at[last - 1], den.at[0, body], sides[0]),
        send(density.at[1], den.at[depth + 3, body], sides[1]),
    ]
    load_d.wait()
    over(0, 1, last, plain(lambda p: faces_x(p, mids)), 0)
    over(1, 1, depth - 2, plain(lambda p: faces_y(p, mids[:-1])), 0)
    pl.semaphore_wait(barrier, len(row_peers) + 2 + inside.astype(jnp.int32) * (1 + beside_y))
    begin(copies)
    field = [
        send(q0.at[last - 1 + 2, body], q0.at[0, body], sides[0]),
        send(q0.at[1 + 2, body], q0.at[depth + 3, body], sides[1]),
    ]

    zero = jnp.zeros((8, 128), F32)
    tell(0)
    load_s.wait()
    over(1, 1, depth - 2, plain(lambda p: inverse(p, mids[1:-1])), 0)
    heard(0)
    tell(1)
    sums = over(2, 1, depth - 4, lambda p, c: first_apply(p, c, mids[2:-2]), (zero, zero, zero))
    arrive(rim_d)

    @pl.when(j == 0)
    def _():
        den[2 : depth + 2, TOP - 8 : TOP] = jnp.zeros((depth, 8, lanes), F32)

    @pl.when(j == ny - 1)
    def _():
        den[2 : depth + 2, end : end + 8] = jnp.zeros((depth, 8, lanes), F32)

    def rims(p):
        faces_y(p, (spans[0], spans[-2], spans[-1]))
        inverse(p, spans[:2] + spans[-2:], rim=False)

    over(0, 1, last, plain(lambda p: faces_x(p, (spans[0], spans[-1]))), 0)
    over(1, last - 2, 2, plain(rims), 0)
    begin(field)
    over(2, 1, depth - 4, plain(rims), 0)
    heard(1)
    tell(2)
    arrive(rim_s)
    over(1, 1, depth - 2, plain(rim_field), 0)
    sums = over(2, 1, depth - 4, lambda p, c: first_apply(p, c, spans[:3] + spans[-3:]), sums)

    arrive(face_d)
    arrive(corner_d)
    for edge, first, there in ((0, i == 0, 0), (nx - 1, i == nx - 1, depth + 2)):
        @pl.when(first)
        def _():
            near = there + 1 if edge == 0 else there
            den[near, TOP - 8 : end + 8] = jnp.zeros((width + 16, lanes), F32)
    for bound, first, rows in ((0, j == 0, TOP - 8), (ny - 1, j == ny - 1, end)):
        @pl.when(first)
        def _():
            den[0:2, rows : rows + 8] = jnp.zeros((2, 8, lanes), F32)
            den[depth + 2 : depth + 4, rows : rows + 8] = jnp.zeros((2, 8, lanes), F32)

    over(-1, depth, 2, plain(faces_x), 0)
    arrive(corner_s)
    over(0, last, 2, plain(whole), 0)
    sums = over(1, last - 2, 2, first_apply, sums)

    arrive(face_s)
    arrive(second_d)
    over(-2, depth + 2, 2, plain(faces_x), 0)

    def outer(p):
        return jnp.logical_or(jnp.logical_and(p < 0, i > 0), jnp.logical_and(p > 0, i < nx - 1))

    over(-1, depth + 1, 2, plain(lambda p: whole(p, outer(p))), 0)
    g0, d0, ss = over(0, last, 2, first_apply, sums)
    h = over(1, 1, depth - 2, second_apply, zero)

    arrive(field)
    over(-1, depth + 1, 2, plain(lambda p: first_apply(p, (None,) * 3, mids, outer(p), False)), 0)
    h = over(0, last, 2, second_apply, h)

    group = lax.broadcasted_iota(jnp.int32, (1, 128), 1) // 32
    row = jnp.zeros((1, 128), F32)
    for k, part in enumerate((g0, d0, ss, h)):
        v = jnp.sum(part, axis=0, keepdims=True)
        v = v + pltpu.roll(v, 64, 1)
        v = v + pltpu.roll(v, 32, 1)
        row = jnp.where(group == k, v, row)

    def spread(k, value, peers, got):
        msg[k] = value
        for s, peer in enumerate(peers):
            pltpu.make_async_remote_copy(
                src_ref=msg.at[k], dst_ref=got.at[s], send_sem=sum_send.at[k], recv_sem=sum_recv.at[k],
                device_id=peer, device_id_type=MESH).start()

    def gathered(k, value, got):
        pltpu.make_async_copy(got, got, sum_recv.at[k]).wait()
        for s in range(got.shape[0]):
            value = value + got[s]
        return value

    spread(0, row, row_peers, got_y)

    def scales(p):
        for r, n in mids:
            rows = pl.ds(r - TOP, n)
            half = 0.5 * inv[p + 1, pl.ds(r, n)]
            scale = half * lax.rsqrt(half)
            scale_out[p, rows] = scale
            t0_out[p, rows] = scale * src[p + 1, pl.ds(r, n)]
            t1_out[p, rows] = scale * t1_out[p, rows]
            t2_out[p, rows] = scale * t2_out[p, rows]

    over(0, 1, depth, plain(scales), 0)
    row = gathered(0, row, got_y)
    heard(2)
    spread(1, row, col_peers, got_x)
    for copy, there, _ in copies:
        pl.when(there)(copy.wait_send)
    row = gathered(1, row, got_x)
    pltpu.make_async_copy(got_y, got_y, sum_send.at[0]).wait()
    pltpu.make_async_copy(got_x, got_x, sum_send.at[1]).wait()

    def total(k):
        return jnp.broadcast_to(jnp.sum(jnp.where(group == k, row, 0.0), axis=1, keepdims=True), (1, 128))

    g0, d0, ss, h = (total(k) for k in range(4))
    alpha0 = g0 / d0
    gamma1 = g0 - 2.0 * alpha0 * d0 + alpha0 * alpha0 * ss
    delta1 = d0 - 2.0 * alpha0 * ss + alpha0 * alpha0 * h
    beta1 = gamma1 / g0
    alpha1 = gamma1 / (delta1 - beta1 * gamma1 / alpha0)
    coef_out[0:1] = alpha0 + alpha1 * (1.0 + beta1)
    coef_out[1:2] = alpha0 * alpha1


def combine(t0, t1, t2, scale, coef, pressure, residual, held_p, held_r, sem):
    a, b = coef[0:1, 0:1], coef[1:2, 0:1]
    copies = []
    for p in range(t0.shape[0]):
        u0, u1 = t0[p], t1[p]
        held_p[p] = scale[p] * (a * u0 - b * u1)
        held_r[p] = u0 - a * u1 + b * t2[p]
        for k, (held, out) in enumerate(((held_p, pressure), (held_r, residual))):
            copies.append(pltpu.make_async_copy(held.at[p], out.at[p], sem.at[k, p]))
            copies[-1].start()
    for copy in copies:
        copy.wait()


def solution(mesh):
    sizes = (mesh.shape["gx"], mesh.shape["gy"])

    def shards(source, density):
        depth, width, lanes = source.shape
        shape = jax.ShapeDtypeStruct(source.shape, F32)

        def planes(n):
            return pltpu.VMEM((n, TOP + width + 16, lanes), F32)

        vmem = pl.BlockSpec(memory_space=pltpu.VMEM)
        hbm = pl.BlockSpec(memory_space=pltpu.HBM)
        t0, t1, t2, scale, coef = pl.pallas_call(
            functools.partial(kernel, sizes),
            out_shape=(shape,) * 4 + (jax.ShapeDtypeStruct((2, 128), F32),),
            in_specs=[hbm] * 2,
            out_specs=(vmem,) * 5,
            scratch_shapes=[
                planes(depth + 4), planes(depth + 2), planes(depth + 4), planes(depth + 2),
                planes(depth + 2), planes(depth + 3), planes(depth + 2), planes(depth + 2),
                pltpu.VMEM((2, 1, 128), F32),
                pltpu.VMEM((2 * sizes[1] - 1, 1, 128), F32),
                pltpu.VMEM((sizes[0] // 2 - 1, 1, 128), F32),
                pltpu.SemaphoreType.DMA((2,)),
                pltpu.SemaphoreType.DMA((20,)),
                pltpu.SemaphoreType.DMA((20,)),
                pltpu.SemaphoreType.DMA((2,)),
                pltpu.SemaphoreType.DMA((2,)),
                pltpu.SemaphoreType.REGULAR((3,)),
            ],
            compiler_params=pltpu.CompilerParams(
                collective_id=1, has_side_effects=True, vmem_limit_bytes=36 * 1024 * 1024),
        )(pltpu.with_memory_space_constraint(source, pltpu.HBM), pltpu.with_memory_space_constraint(density, pltpu.HBM))
        pressure, residual = pl.pallas_call(
            combine,
            out_shape=(shape, shape),
            in_specs=[vmem] * 5,
            out_specs=(hbm, hbm),
            scratch_shapes=[
                pltpu.VMEM(source.shape, F32), pltpu.VMEM(source.shape, F32), pltpu.SemaphoreType.DMA((2, depth))],
            compiler_params=pltpu.CompilerParams(vmem_limit_bytes=16 * 1024 * 1024),
        )(t0, t1, t2, scale, coef)
        return pressure, residual

    spec = P("gx", "gy", None)
    return jax.shard_map(shards, mesh=mesh, in_specs=(spec, spec), out_specs=(spec, spec), check_vma=False)
```

```python
import functools

import jax
import jax.numpy as jnp
from jax import lax
from jax.experimental import pallas as pl
from jax.experimental.pallas import tpu as pltpu
from jax.sharding import PartitionSpec as P

MESH = pl.DeviceIdType.MESH
F32 = jnp.float32
TOP = 16


def recip(x):
    r = pl.reciprocal(x, approx=True)
    return r * (2.0 - x * r)


def fold(v):
    rows, lanes = v.shape
    out = None
    for r in range(0, rows, 8):
        for c in range(0, lanes, 128):
            piece = v[r : r + 8, c : c + 128]
            out = piece if out is None else out + piece
    return out


def kernel(sizes, source, density, t0_out, t1_out, t2_out, scale_out, coef_out,
           den, src, q0, q1, inv, wx, wy, wz, msg, got_y, got_x,
           local_sem, send_sem, recv_sem, sum_send, sum_recv, known):
    nx, ny = sizes
    depth, width, lanes = t1_out.shape
    end = TOP + width
    last = depth - 1
    i, j = lax.axis_index("gx"), lax.axis_index("gy")
    right, left = (i + 1, i < nx - 1, i > 0), (i - 1, i > 0, i < nx - 1)
    above, below = (j + 1, j < ny - 1, j > 0), (j - 1, j > 0, j < ny - 1)

    def beside(a, b):
        both = jnp.logical_and
        return ((a[0], b[0]), both(a[1], b[1]), both(a[2], b[2]))

    sides = [((right[0], j), right[1], right[2]), ((left[0], j), left[1], left[2])]
    side = int(ny**0.5)
    chips = nx // 2
    core = lax.rem(i, 2)

    def far(k, n):
        return min(k, n - k)

    offsets = [(b, a, c) for b in range(side) for a in range(side) for c in range(2)][1:]
    offsets.sort(key=lambda o: -far(o[0], side) - far(o[1], side))
    row_peers = [
        (i + c * (1 - 2 * core), lax.rem(j // side + b, side) * side + lax.rem(lax.rem(j, side) + a, side))
        for b, a, c in offsets
    ]
    col_peers = [
        (lax.rem(i + 2 * k, nx), j) for k in sorted(range(1, chips), key=lambda k: -far(k, chips))
    ]
    corners = [beside(a, b) for a in (right, left) for b in (above, below)]

    body, low, high = pl.ds(TOP, width), pl.ds(TOP - 8, 8), pl.ds(end, 8)
    load_d = pltpu.make_async_copy(density, den.at[pl.ds(2, depth), body], local_sem.at[0])
    load_s = pltpu.make_async_copy(source, src.at[pl.ds(1, depth), body], local_sem.at[1])
    load_d.start()
    load_s.start()

    barrier = pltpu.get_barrier_semaphore()
    across = i + 2 * core - 1
    inside = jnp.logical_and(across >= 0, across < nx)
    for row, there in ((j, True), (j + 1, j < ny - 1), (j - 1, j > 0)):
        @pl.when(jnp.logical_and(inside, there))
        def _():
            pl.semaphore_signal(barrier, inc=1, device_id=(across, row), device_id_type=MESH)
    for peer in [(lax.rem(i + 2, nx), j), (lax.rem(i + nx - 2, nx), j)] + row_peers[::-1]:
        pl.semaphore_signal(barrier, inc=1, device_id=peer, device_id_type=MESH)
    beside_y = (j > 0).astype(jnp.int32) + (j < ny - 1).astype(jnp.int32)

    rounds = (chips - 1).bit_length() - 1

    def tell(k):
        if k < rounds:
            for step in (2 ** (k + 1), nx - 2 ** (k + 1)):
                pl.semaphore_signal(
                    known.at[k], inc=1, device_id=(lax.rem(i + step, nx), j), device_id_type=MESH)

    def heard(k):
        if k < rounds:
            pl.semaphore_wait(known.at[k], 2)

    def arrive(group):
        for copy, _, opposite in group:
            pl.when(opposite)(copy.wait_recv)

    mids = [(r, 16) for r in range(TOP, end, 16)]
    spans = [(TOP - 8, 8)] + mids + [(end, 8)]

    def keep_y(r, v):
        if r < TOP:
            return jnp.where(j > 0, v, 0.0)
        if r >= end:
            return jnp.where(j < ny - 1, v, 0.0)
        return v

    def faces_x(p, rows=spans):
        for r, n in rows:
            wx[p + 2, pl.ds(r, n)] = recip(den[p + 2, pl.ds(r, n)] + den[p + 3, pl.ds(r, n)])

    def faces_y(p, rows=spans):
        for r, n in rows:
            wy[p + 1, pl.ds(r, n)] = recip(den[p + 2, pl.ds(r, n)] + den[p + 2, pl.ds(r + 1, n)])

    def in_plane_faces(p, r, n):
        d = den[p + 2, pl.ds(r, n)]
        lane = lax.broadcasted_iota(jnp.int32, (n, lanes), 1)
        beyond = jnp.where(lane == lanes - 1, 0.0, pltpu.roll(d, lanes - 1, 1))
        ahead = recip(d + beyond)
        wz[p + 1, pl.ds(r, n)] = jnp.where(lane == lanes - 1, 0.0, ahead)
        behind = jnp.where(lane == 0, recip(d), pltpu.roll(ahead, 1, 1))
        return wy[p + 1, pl.ds(r, n)] + wy[p + 1, pl.ds(r - 1, n)] + ahead + behind

    def inverse(p, rows=spans, rim=True):
        for r, n in rows:
            diag = in_plane_faces(p, r, n) + wx[p + 2, pl.ds(r, n)] + wx[p + 1, pl.ds(r, n)]
            b = recip(diag)
            inv[p + 1, pl.ds(r, n)] = b
            if rim or TOP <= r < end:
                q0[p + 2, pl.ds(r, n)] = keep_y(r, b * src[p + 1, pl.ds(r, n)])

    def rim_field(p):
        for r, n in (spans[0], spans[-1]):
            q0[p + 2, pl.ds(r, n)] = keep_y(r, inv[p + 1, pl.ds(r, n)] * src[p + 1, pl.ds(r, n)])

    def in_plane(v, shift, p, r, n):
        mid = v[p + shift, pl.ds(r, n)]
        total = wy[p + 1, pl.ds(r, n)] * v[p + shift, pl.ds(r + 1, n)]
        total = total + wy[p + 1, pl.ds(r - 1, n)] * v[p + shift, pl.ds(r - 1, n)]
        w = wz[p + 1, pl.ds(r, n)]
        total = total + w * pltpu.roll(mid, lanes - 1, 1)
        return mid, total + pltpu.roll(w * mid, 1, 1)

    def coupled(v, shift, p, r, n):
        mid, total = in_plane(v, shift, p, r, n)
        total = total + wx[p + 2, pl.ds(r, n)] * v[p + shift + 1, pl.ds(r, n)]
        return mid, total + wx[p + 1, pl.ds(r, n)] * v[p + shift - 1, pl.ds(r, n)]

    def first_apply(p, sums, rows=spans):
        g0, d0, ss = sums
        for r, n in rows:
            mid, total = coupled(q0, 2, p, r, n)
            s = src[p + 1, pl.ds(r, n)]
            t = s - total
            q = keep_y(r, inv[p + 1, pl.ds(r, n)] * t)
            q1[p + 1, pl.ds(r, n)] = q
            if TOP <= r < end:
                t1_out[p, pl.ds(r - TOP, n)] = t
                g0 = g0 + fold(s * mid)
                d0 = d0 + fold(t * mid)
                ss = ss + fold(t * q)
        return g0, d0, ss

    def second_apply(p, h):
        for r, n in mids:
            mid, total = coupled(q1, 1, p, r, n)
            t = t1_out[p, pl.ds(r - TOP, n)] - total
            t2_out[p, pl.ds(r - TOP, n)] = t
            h = h + fold(t * mid)
        return h

    def at_end(k):
        return depth * k + k - 1, last * k, 1 + (last - 2) * k, 1 + depth * k, (depth + 2) * k, 2 + (last - 1) * k

    def beyond_of(k):
        return (depth + 3) * k

    def present(k):
        return jnp.where(k == 0, i, nx - 1 - i) > 0

    def own_weights(k):
        _, own, _, _, _, inner = at_end(k)
        faces_y(own)
        for r, n in spans:
            inv[own + 1, pl.ds(r, n)] = in_plane_faces(own, r, n) + wx[inner, pl.ds(r, n)]

    def own_field(k):
        out, own, _, face, _, _ = at_end(k)
        for r, n in spans:
            rows = pl.ds(r, n)
            w = recip(den[out + 2, rows] + den[own + 2, rows])
            wx[face, rows] = w
            b = recip(inv[own + 1, rows] + w)
            inv[own + 1, rows] = b
            q0[own + 2, rows] = keep_y(r, b * src[own + 1, rows])

    def end_weights(k):
        out, own, nxt, face, _, inner = at_end(k)
        faces_y(out)
        for r, n in spans:
            rows = pl.ds(r, n)
            inv[out + 1, rows] = in_plane_faces(out, r, n) + wx[face, rows]
            mid, total = in_plane(q0, 2, own, r, n)
            q1[own + 1, rows] = src[own + 1, rows] - total - wx[inner, rows] * q0[nxt + 2, rows]

    def end_field(k, sums):
        out, own, _, face, outer, _ = at_end(k)
        g0, d0, ss = sums
        for r, n in spans:
            rows = pl.ds(r, n)
            w = recip(den[out + 2, rows] + den[beyond_of(k), rows])
            wx[outer, rows] = w
            b = recip(inv[out + 1, rows] + w)
            inv[out + 1, rows] = b
            q = jnp.where(present(k), keep_y(r, b * src[out + 1, rows]), 0.0)
            q0[out + 2, rows] = q
            t = q1[own + 1, rows] - wx[face, rows] * q
            q = keep_y(r, inv[own + 1, rows] * t)
            q1[own + 1, rows] = q
            if TOP <= r < end:
                s, mid = src[own + 1, rows], q0[own + 2, rows]
                t1_out[own, pl.ds(r - TOP, n)] = t
                g0 = g0 + fold(s * mid)
                d0 = d0 + fold(t * mid)
                ss = ss + fold(t * q)
        return g0, d0, ss

    def end_second(k, h):
        out, own, nxt, face, _, inner = at_end(k)
        for r, n in mids:
            rows = pl.ds(r, n)
            _, total = in_plane(q0, 2, out, r, n)
            q1[out + 1, rows] = src[out + 1, rows] - total - wx[face, rows] * q0[own + 2, rows]
            mid, total = in_plane(q1, 1, own, r, n)
            t = t1_out[own, pl.ds(r - TOP, n)] - total - wx[inner, rows] * q1[nxt + 1, rows]
            t2_out[own, pl.ds(r - TOP, n)] = t
            h = h + fold(t * mid)
        return h

    def end_last(k, rows_of, h):
        out, own, _, face, outer, _ = at_end(k)
        for r, n in rows_of:
            rows = pl.ds(r, n)
            t = q1[out + 1, rows] - wx[outer, rows] * q0[beyond_of(k), rows]
            q = jnp.where(present(k), inv[out + 1, rows] * t, 0.0)
            c = wx[face, rows] * q
            t2_out[own, pl.ds(r - TOP, n)] = t2_out[own, pl.ds(r - TOP, n)] - c
            if h is not None:
                h = h - 2.0 * fold(c * q1[own + 1, rows])
        return h

    def over(start, step, count, f, carry=None):
        def go(k, c):
            return f(start + step * k, c)
        return lax.fori_loop(0, count, go, carry)

    def plain(f):
        def g(p, c):
            f(p)
            return c
        return g

    copies = []

    def send(what, where, peer):
        k = len(copies)
        who, there, opposite = peer
        copies.append((pltpu.make_async_remote_copy(
            src_ref=what, dst_ref=where, send_sem=send_sem.at[k], recv_sem=recv_sem.at[k],
            device_id=who, device_id_type=MESH), there, opposite))
        return copies[-1]

    def begin(group):
        for copy, there, _ in group:
            pl.when(there)(copy.start)

    own_d, own_s = pl.ds(2, depth), pl.ds(1, depth)

    def ends(n):
        return ((above, pl.ds(width - n, n), pl.ds(TOP - n, n)), (below, pl.ds(0, n), pl.ds(end, n)))

    rim_d = [send(density.at[:, rows], den.at[own_d, place], ((i, b[0]), b[1], b[2])) for b, rows, place in ends(3)]
    face_d = [
        send(density.at[last], den.at[1, body], sides[0]),
        send(density.at[0], den.at[depth + 2, body], sides[1]),
    ]
    rim_s = [send(source.at[:, rows], src.at[own_s, place], ((i, b[0]), b[1], b[2])) for b, rows, place in ends(2)]
    corner_d, corner_s = [], []
    for a in (right, left):
        plane, there = (last - 1, 0) if a is right else (0, depth + 2)
        face, face_there = (last, 0) if a is right else (0, depth + 1)
        for b, rows, place in ends(2):
            corner_d.append(send(density.at[pl.ds(plane, 2), rows], den.at[pl.ds(there, 2), place], beside(a, b)))
        for b, rows, place in ends(1):
            corner_s.append(send(source.at[face, rows], src.at[face_there, place], beside(a, b)))
    face_s = [
        send(source.at[last], src.at[0, body], sides[0]),
        send(source.at[0], src.at[depth + 1, body], sides[1]),
    ]
    second_d = [
        send(density.at[last - 1], den.at[0, body], sides[0]),
        send(density.at[1], den.at[depth + 3, body], sides[1]),
    ]
    load_d.wait()
    over(0, 1, last, plain(lambda p: faces_x(p, mids)), 0)
    over(1, 1, depth - 2, plain(lambda p: faces_y(p, mids[:-1])), 0)
    pl.semaphore_wait(barrier, len(row_peers) + 2 + inside.astype(jnp.int32) * (1 + beside_y))
    begin(copies)
    half = width // 2
    lower, upper = pl.ds(TOP, half), pl.ds(TOP + half, half)
    field, field_later = (
        [
            send(q0.at[last + 1, a], q0.at[0, a], sides[0]),
            send(q0.at[3, b], q0.at[depth + 3, b], sides[1]),
        ]
        for a, b in ((upper, lower), (lower, upper))
    )

    zero = jnp.zeros((8, 128), F32)
    tell(0)
    load_s.wait()
    over(1, 1, depth - 2, plain(lambda p: inverse(p, mids[1:-1])), 0)
    heard(0)
    tell(1)
    sums = over(2, 1, depth - 4, lambda p, c: first_apply(p, c, mids[2:-2]), (zero, zero, zero))
    arrive(rim_d)

    @pl.when(j == 0)
    def _():
        den[2 : depth + 2, TOP - 8 : TOP] = jnp.zeros((depth, 8, lanes), F32)

    @pl.when(j == ny - 1)
    def _():
        den[2 : depth + 2, end : end + 8] = jnp.zeros((depth, 8, lanes), F32)

    def rims(p):
        faces_y(p, (spans[0], spans[-2], spans[-1]))
        inverse(p, spans[:2] + spans[-2:], rim=False)

    over(0, 1, last, plain(lambda p: faces_x(p, (spans[0], spans[-1]))), 0)
    over(1, last - 2, 2, plain(rims), 0)
    begin(field)
    begin(field_later)
    over(2, 1, depth - 4, plain(rims), 0)
    heard(1)
    tell(2)
    arrive(rim_s)
    over(1, 1, depth - 2, plain(rim_field), 0)
    sums = over(2, 1, depth - 4, lambda p, c: first_apply(p, c, spans[:3] + spans[-3:]), sums)

    over(0, 1, 2, plain(own_weights), 0)
    h = over(3, 1, depth - 6, second_apply, zero)
    arrive(face_d)
    arrive(corner_d)
    for edge, first, there in ((0, i == 0, 0), (nx - 1, i == nx - 1, depth + 2)):
        @pl.when(first)
        def _():
            near = there + 1 if edge == 0 else there
            den[near, TOP - 8 : end + 8] = jnp.zeros((width + 16, lanes), F32)
    for bound, first, rows in ((0, j == 0, TOP - 8), (ny - 1, j == ny - 1, end)):
        @pl.when(first)
        def _():
            den[0:2, rows : rows + 8] = jnp.zeros((2, 8, lanes), F32)
            den[depth + 2 : depth + 4, rows : rows + 8] = jnp.zeros((2, 8, lanes), F32)

    arrive(corner_s)
    over(0, 1, 2, plain(own_field), 0)
    sums = over(1, last - 2, 2, first_apply, sums)
    over(0, 1, 2, plain(end_weights), 0)
    h = over(2, depth - 5, 2, second_apply, h)

    arrive(face_s)
    arrive(second_d)
    g0, d0, ss = over(0, 1, 2, end_field, sums)
    h = over(0, 1, 2, end_second, h)
    h = over(1, last - 2, 2, second_apply, h)

    arrive(field)
    low_half, high_half = mids[: half // 16], mids[half // 16 :]
    h = end_last(1, low_half, end_last(0, high_half, h))

    group = lax.broadcasted_iota(jnp.int32, (1, 128), 1) // 32
    row = jnp.zeros((1, 128), F32)
    for k, part in enumerate((g0, d0, ss, h)):
        v = jnp.sum(part, axis=0, keepdims=True)
        v = v + pltpu.roll(v, 64, 1)
        v = v + pltpu.roll(v, 32, 1)
        row = jnp.where(group == k, v, row)

    def spread(k, value, peers, got):
        msg[k] = value
        for s, peer in enumerate(peers):
            pltpu.make_async_remote_copy(
                src_ref=msg.at[k], dst_ref=got.at[s], send_sem=sum_send.at[k], recv_sem=sum_recv.at[k],
                device_id=peer, device_id_type=MESH).start()

    def gathered(k, value, got):
        pltpu.make_async_copy(got, got, sum_recv.at[k]).wait()
        for s in range(got.shape[0]):
            value = value + got[s]
        return value

    spread(0, row, row_peers, got_y)

    def scales(p):
        for r, n in mids:
            rows = pl.ds(r - TOP, n)
            half = 0.5 * inv[p + 1, pl.ds(r, n)]
            scale = half * lax.rsqrt(half)
            scale_out[p, rows] = scale
            t0_out[p, rows] = scale * src[p + 1, pl.ds(r, n)]
            t1_out[p, rows] = scale * t1_out[p, rows]
            t2_out[p, rows] = scale * t2_out[p, rows]

    arrive(field_later)
    end_last(0, low_half, None)
    end_last(1, high_half, None)
    over(0, 1, depth, plain(scales), 0)
    row = gathered(0, row, got_y)
    heard(2)
    spread(1, row, col_peers, got_x)
    for copy, there, _ in copies:
        pl.when(there)(copy.wait_send)
    row = gathered(1, row, got_x)
    pltpu.make_async_copy(got_y, got_y, sum_send.at[0]).wait()
    pltpu.make_async_copy(got_x, got_x, sum_send.at[1]).wait()

    def total(k):
        return jnp.broadcast_to(jnp.sum(jnp.where(group == k, row, 0.0), axis=1, keepdims=True), (1, 128))

    g0, d0, ss, h = (total(k) for k in range(4))
    alpha0 = g0 / d0
    gamma1 = g0 - 2.0 * alpha0 * d0 + alpha0 * alpha0 * ss
    delta1 = d0 - 2.0 * alpha0 * ss + alpha0 * alpha0 * h
    beta1 = gamma1 / g0
    alpha1 = gamma1 / (delta1 - beta1 * gamma1 / alpha0)
    coef_out[0:1] = alpha0 + alpha1 * (1.0 + beta1)
    coef_out[1:2] = alpha0 * alpha1


def combine(t0, t1, t2, scale, coef, pressure, residual, held_p, held_r, sem):
    a, b = coef[0:1, 0:1], coef[1:2, 0:1]
    copies = []
    for p in range(t0.shape[0]):
        u0, u1 = t0[p], t1[p]
        held_p[p] = scale[p] * (a * u0 - b * u1)
        held_r[p] = u0 - a * u1 + b * t2[p]
        for k, (held, out) in enumerate(((held_p, pressure), (held_r, residual))):
            copies.append(pltpu.make_async_copy(held.at[p], out.at[p], sem.at[k, p]))
            copies[-1].start()
    for copy in copies:
        copy.wait()


def solution(mesh):
    sizes = (mesh.shape["gx"], mesh.shape["gy"])

    def shards(source, density):
        depth, width, lanes = source.shape
        shape = jax.ShapeDtypeStruct(source.shape, F32)

        def planes(n):
            return pltpu.VMEM((n, TOP + width + 16, lanes), F32)

        vmem = pl.BlockSpec(memory_space=pltpu.VMEM)
        hbm = pl.BlockSpec(memory_space=pltpu.HBM)
        t0, t1, t2, scale, coef = pl.pallas_call(
            functools.partial(kernel, sizes),
            out_shape=(shape,) * 4 + (jax.ShapeDtypeStruct((2, 128), F32),),
            in_specs=[hbm] * 2,
            out_specs=(vmem,) * 5,
            scratch_shapes=[
                planes(depth + 4), planes(depth + 2), planes(depth + 4), planes(depth + 2),
                planes(depth + 2), planes(depth + 3), planes(depth + 2), planes(depth + 2),
                pltpu.VMEM((2, 1, 128), F32),
                pltpu.VMEM((2 * sizes[1] - 1, 1, 128), F32),
                pltpu.VMEM((sizes[0] // 2 - 1, 1, 128), F32),
                pltpu.SemaphoreType.DMA((2,)),
                pltpu.SemaphoreType.DMA((22,)),
                pltpu.SemaphoreType.DMA((22,)),
                pltpu.SemaphoreType.DMA((2,)),
                pltpu.SemaphoreType.DMA((2,)),
                pltpu.SemaphoreType.REGULAR((3,)),
            ],
            compiler_params=pltpu.CompilerParams(
                collective_id=1, has_side_effects=True, vmem_limit_bytes=36 * 1024 * 1024),
        )(pltpu.with_memory_space_constraint(source, pltpu.HBM), pltpu.with_memory_space_constraint(density, pltpu.HBM))
        pressure, residual = pl.pallas_call(
            combine,
            out_shape=(shape, shape),
            in_specs=[vmem] * 5,
            out_specs=(hbm, hbm),
            scratch_shapes=[
                pltpu.VMEM(source.shape, F32), pltpu.VMEM(source.shape, F32), pltpu.SemaphoreType.DMA((2, depth))],
            compiler_params=pltpu.CompilerParams(vmem_limit_bytes=16 * 1024 * 1024),
        )(t0, t1, t2, scale, coef)
        return pressure, residual

    spec = P("gx", "gy", None)
    return jax.shard_map(shards, mesh=mesh, in_specs=(spec, spec), out_specs=(spec, spec), check_vma=False)
```

```python
import functools

import jax
import jax.numpy as jnp
from jax import lax
from jax.experimental import pallas as pl
from jax.experimental.pallas import tpu as pltpu
from jax.sharding import PartitionSpec as P

MESH = pl.DeviceIdType.MESH
F32 = jnp.float32
TOP = 16


def recip(x):
    r = pl.reciprocal(x, approx=True)
    return r * (2.0 - x * r)


def fold(v):
    rows, lanes = v.shape
    out = None
    for r in range(0, rows, 8):
        for c in range(0, lanes, 128):
            piece = v[r : r + 8, c : c + 128]
            out = piece if out is None else out + piece
    return out


def kernel(sizes, source, density, t0_out, t1_out, t2_out, scale_out, coef_out,
           den, src, q0, q1, inv, wx, wy, wz, msg, got_y, got_x,
           local_sem, send_sem, recv_sem, sum_send, sum_recv, known):
    nx, ny = sizes
    depth, width, lanes = t1_out.shape
    end = TOP + width
    last = depth - 1
    i, j = lax.axis_index("gx"), lax.axis_index("gy")
    right, left = (i + 1, i < nx - 1, i > 0), (i - 1, i > 0, i < nx - 1)
    above, below = (j + 1, j < ny - 1, j > 0), (j - 1, j > 0, j < ny - 1)

    def beside(a, b):
        both = jnp.logical_and
        return ((a[0], b[0]), both(a[1], b[1]), both(a[2], b[2]))

    sides = [((right[0], j), right[1], right[2]), ((left[0], j), left[1], left[2])]
    side = int(ny**0.5)
    chips = nx // 2
    core = lax.rem(i, 2)

    def far(k, n):
        return min(k, n - k)

    offsets = [(b, a, c) for b in range(side) for a in range(side) for c in range(2)][1:]
    offsets.sort(key=lambda o: -far(o[0], side) - far(o[1], side))
    row_peers = [
        (i + c * (1 - 2 * core), lax.rem(j // side + b, side) * side + lax.rem(lax.rem(j, side) + a, side))
        for b, a, c in offsets
    ]
    col_peers = [
        (lax.rem(i + 2 * k, nx), j) for k in sorted(range(1, chips), key=lambda k: -far(k, chips))
    ]
    corners = [beside(a, b) for a in (right, left) for b in (above, below)]

    body, low, high = pl.ds(TOP, width), pl.ds(TOP - 8, 8), pl.ds(end, 8)
    load_d = pltpu.make_async_copy(density, den.at[pl.ds(2, depth), body], local_sem.at[0])
    load_s = pltpu.make_async_copy(source, src.at[pl.ds(1, depth), body], local_sem.at[1])
    load_d.start()
    load_s.start()

    barrier = pltpu.get_barrier_semaphore()
    across = i + 2 * core - 1
    inside = jnp.logical_and(across >= 0, across < nx)
    for row, there in ((j, True), (j + 1, j < ny - 1), (j - 1, j > 0)):
        @pl.when(jnp.logical_and(inside, there))
        def _():
            pl.semaphore_signal(barrier, inc=1, device_id=(across, row), device_id_type=MESH)
    for peer in [(lax.rem(i + 2, nx), j), (lax.rem(i + nx - 2, nx), j)] + row_peers[::-1]:
        pl.semaphore_signal(barrier, inc=1, device_id=peer, device_id_type=MESH)
    beside_y = (j > 0).astype(jnp.int32) + (j < ny - 1).astype(jnp.int32)

    rounds = (chips - 1).bit_length() - 1

    def tell(k):
        if k < rounds:
            for step in (2 ** (k + 1), nx - 2 ** (k + 1)):
                pl.semaphore_signal(
                    known.at[k], inc=1, device_id=(lax.rem(i + step, nx), j), device_id_type=MESH)

    def heard(k):
        if k < rounds:
            pl.semaphore_wait(known.at[k], 2)

    def arrive(group):
        for copy, _, opposite in group:
            pl.when(opposite)(copy.wait_recv)

    mids = [(r, 16) for r in range(TOP, end, 16)]
    spans = [(TOP - 8, 8)] + mids + [(end, 8)]

    def keep_y(r, v):
        if r < TOP:
            return jnp.where(j > 0, v, 0.0)
        if r >= end:
            return jnp.where(j < ny - 1, v, 0.0)
        return v

    def faces_x(p, rows=spans):
        for r, n in rows:
            wx[p + 2, pl.ds(r, n)] = recip(den[p + 2, pl.ds(r, n)] + den[p + 3, pl.ds(r, n)])

    def faces_y(p, rows=spans):
        for r, n in rows:
            wy[p + 1, pl.ds(r, n)] = recip(den[p + 2, pl.ds(r, n)] + den[p + 2, pl.ds(r + 1, n)])

    def in_plane_faces(p, r, n):
        d = den[p + 2, pl.ds(r, n)]
        lane = lax.broadcasted_iota(jnp.int32, (n, lanes), 1)
        beyond = jnp.where(lane == lanes - 1, 0.0, pltpu.roll(d, lanes - 1, 1))
        ahead = recip(d + beyond)
        wz[p + 1, pl.ds(r, n)] = jnp.where(lane == lanes - 1, 0.0, ahead)
        behind = jnp.where(lane == 0, recip(d), pltpu.roll(ahead, 1, 1))
        return wy[p + 1, pl.ds(r, n)] + wy[p + 1, pl.ds(r - 1, n)] + ahead + behind

    def inverse(p, rows=spans, rim=True):
        for r, n in rows:
            diag = in_plane_faces(p, r, n) + wx[p + 2, pl.ds(r, n)] + wx[p + 1, pl.ds(r, n)]
            b = recip(diag)
            inv[p + 1, pl.ds(r, n)] = b
            if rim or TOP <= r < end:
                q0[p + 2, pl.ds(r, n)] = keep_y(r, b * src[p + 1, pl.ds(r, n)])

    def rim_field(p):
        for r, n in (spans[0], spans[-1]):
            q0[p + 2, pl.ds(r, n)] = keep_y(r, inv[p + 1, pl.ds(r, n)] * src[p + 1, pl.ds(r, n)])

    def in_plane(v, shift, p, r, n):
        mid = v[p + shift, pl.ds(r, n)]
        total = wy[p + 1, pl.ds(r, n)] * v[p + shift, pl.ds(r + 1, n)]
        total = total + wy[p + 1, pl.ds(r - 1, n)] * v[p + shift, pl.ds(r - 1, n)]
        w = wz[p + 1, pl.ds(r, n)]
        total = total + w * pltpu.roll(mid, lanes - 1, 1)
        return mid, total + pltpu.roll(w * mid, 1, 1)

    def coupled(v, shift, p, r, n):
        mid, total = in_plane(v, shift, p, r, n)
        total = total + wx[p + 2, pl.ds(r, n)] * v[p + shift + 1, pl.ds(r, n)]
        return mid, total + wx[p + 1, pl.ds(r, n)] * v[p + shift - 1, pl.ds(r, n)]

    def first_apply(p, sums, rows=spans):
        g0, d0, ss = sums
        for r, n in rows:
            mid, total = coupled(q0, 2, p, r, n)
            s = src[p + 1, pl.ds(r, n)]
            t = s - total
            q = keep_y(r, inv[p + 1, pl.ds(r, n)] * t)
            q1[p + 1, pl.ds(r, n)] = q
            if TOP <= r < end:
                t1_out[p, pl.ds(r - TOP, n)] = t
                g0 = g0 + fold(s * mid)
                d0 = d0 + fold(t * mid)
                ss = ss + fold(t * q)
        return g0, d0, ss

    def second_apply(p, h):
        for r, n in mids:
            mid, total = coupled(q1, 1, p, r, n)
            t = t1_out[p, pl.ds(r - TOP, n)] - total
            t2_out[p, pl.ds(r - TOP, n)] = t
            h = h + fold(t * mid)
        return h

    def at_end(k):
        return depth * k + k - 1, last * k, 1 + (last - 2) * k, 1 + depth * k, (depth + 2) * k, 2 + (last - 1) * k

    def beyond_of(k):
        return (depth + 3) * k

    def present(k):
        return jnp.where(k == 0, i, nx - 1 - i) > 0

    def own_weights(k):
        _, own, _, _, _, inner = at_end(k)
        faces_y(own)
        for r, n in spans:
            inv[own + 1, pl.ds(r, n)] = in_plane_faces(own, r, n) + wx[inner, pl.ds(r, n)]

    def own_field(k):
        out, own, _, face, _, _ = at_end(k)
        for r, n in spans:
            rows = pl.ds(r, n)
            w = recip(den[out + 2, rows] + den[own + 2, rows])
            wx[face, rows] = w
            b = recip(inv[own + 1, rows] + w)
            inv[own + 1, rows] = b
            q0[own + 2, rows] = keep_y(r, b * src[own + 1, rows])

    def end_weights(k):
        out, own, nxt, face, _, inner = at_end(k)
        faces_y(out)
        for r, n in spans:
            rows = pl.ds(r, n)
            inv[out + 1, rows] = in_plane_faces(out, r, n) + wx[face, rows]
            mid, total = in_plane(q0, 2, own, r, n)
            q1[own + 1, rows] = src[own + 1, rows] - total - wx[inner, rows] * q0[nxt + 2, rows]

    def end_field(k, sums):
        out, own, _, face, outer, _ = at_end(k)
        g0, d0, ss = sums
        for r, n in spans:
            rows = pl.ds(r, n)
            w = recip(den[out + 2, rows] + den[beyond_of(k), rows])
            wx[outer, rows] = w
            b = recip(inv[out + 1, rows] + w)
            inv[out + 1, rows] = b
            q = jnp.where(present(k), keep_y(r, b * src[out + 1, rows]), 0.0)
            q0[out + 2, rows] = q
            t = q1[own + 1, rows] - wx[face, rows] * q
            q = keep_y(r, inv[own + 1, rows] * t)
            q1[own + 1, rows] = q
            if TOP <= r < end:
                s, mid = src[own + 1, rows], q0[own + 2, rows]
                t1_out[own, pl.ds(r - TOP, n)] = t
                g0 = g0 + fold(s * mid)
                d0 = d0 + fold(t * mid)
                ss = ss + fold(t * q)
        return g0, d0, ss

    def end_second(k, h):
        out, own, nxt, face, _, inner = at_end(k)
        for r, n in mids:
            rows = pl.ds(r, n)
            _, total = in_plane(q0, 2, out, r, n)
            q1[out + 1, rows] = src[out + 1, rows] - total - wx[face, rows] * q0[own + 2, rows]
            mid, total = in_plane(q1, 1, own, r, n)
            t = t1_out[own, pl.ds(r - TOP, n)] - total - wx[inner, rows] * q1[nxt + 1, rows]
            t2_out[own, pl.ds(r - TOP, n)] = t
            h = h + fold(t * mid)
        return h

    def end_last(k, rows_of, h):
        out, own, _, face, outer, _ = at_end(k)
        for r, n in rows_of:
            rows = pl.ds(r, n)
            t = q1[out + 1, rows] - wx[outer, rows] * q0[beyond_of(k), rows]
            q = jnp.where(present(k), inv[out + 1, rows] * t, 0.0)
            c = wx[face, rows] * q
            t2_out[own, pl.ds(r - TOP, n)] = t2_out[own, pl.ds(r - TOP, n)] - c
            if h is not None:
                h = h - 2.0 * fold(c * q1[own + 1, rows])
        return h

    def over(start, step, count, f, carry=None):
        def go(k, c):
            return f(start + step * k, c)
        return lax.fori_loop(0, count, go, carry)

    def plain(f):
        def g(p, c):
            f(p)
            return c
        return g

    copies = []

    def send(what, where, peer):
        k = len(copies)
        who, there, opposite = peer
        copies.append((pltpu.make_async_remote_copy(
            src_ref=what, dst_ref=where, send_sem=send_sem.at[k], recv_sem=recv_sem.at[k],
            device_id=who, device_id_type=MESH), there, opposite))
        return copies[-1]

    def begin(group):
        for copy, there, _ in group:
            pl.when(there)(copy.start)

    own_d, own_s = pl.ds(2, depth), pl.ds(1, depth)

    def ends(n):
        return ((above, pl.ds(width - n, n), pl.ds(TOP - n, n)), (below, pl.ds(0, n), pl.ds(end, n)))

    rim_d = [send(density.at[:, rows], den.at[own_d, place], ((i, b[0]), b[1], b[2])) for b, rows, place in ends(3)]
    face_d = [
        send(density.at[last], den.at[1, body], sides[0]),
        send(density.at[0], den.at[depth + 2, body], sides[1]),
    ]
    rim_s = [send(source.at[:, rows], src.at[own_s, place], ((i, b[0]), b[1], b[2])) for b, rows, place in ends(2)]
    corner_d, corner_s = [], []
    for a in (right, left):
        plane, there = (last - 1, 0) if a is right else (0, depth + 2)
        face, face_there = (last, 0) if a is right else (0, depth + 1)
        for b, rows, place in ends(2):
            corner_d.append(send(density.at[pl.ds(plane, 2), rows], den.at[pl.ds(there, 2), place], beside(a, b)))
        for b, rows, place in ends(1):
            corner_s.append(send(source.at[face, rows], src.at[face_there, place], beside(a, b)))
    face_s = [
        send(source.at[last], src.at[0, body], sides[0]),
        send(source.at[0], src.at[depth + 1, body], sides[1]),
    ]
    second_d = [
        send(density.at[last - 1], den.at[0, body], sides[0]),
        send(density.at[1], den.at[depth + 3, body], sides[1]),
    ]
    load_d.wait()
    over(0, 1, last, plain(lambda p: faces_x(p, mids)), 0)
    over(1, 1, depth - 2, plain(lambda p: faces_y(p, mids[:-1])), 0)
    pl.semaphore_wait(barrier, len(row_peers) + 2 + inside.astype(jnp.int32) * (1 + beside_y))
    begin(rim_d + rim_s + corner_d + corner_s + face_d + face_s + second_d)
    half = width // 2
    lower, upper = pl.ds(TOP, half), pl.ds(TOP + half, half)
    field, field_later = (
        [
            send(q0.at[last + 1, a], q0.at[0, a], sides[0]),
            send(q0.at[3, b], q0.at[depth + 3, b], sides[1]),
        ]
        for a, b in ((upper, lower), (lower, upper))
    )

    zero = jnp.zeros((8, 128), F32)
    tell(0)
    load_s.wait()
    over(1, 1, depth - 2, plain(lambda p: inverse(p, mids[1:-1])), 0)
    heard(0)
    tell(1)
    sums = over(2, 1, depth - 4, lambda p, c: first_apply(p, c, mids[2:-2]), (zero, zero, zero))
    arrive(rim_d)

    @pl.when(j == 0)
    def _():
        den[2 : depth + 2, TOP - 8 : TOP] = jnp.zeros((depth, 8, lanes), F32)

    @pl.when(j == ny - 1)
    def _():
        den[2 : depth + 2, end : end + 8] = jnp.zeros((depth, 8, lanes), F32)

    def rims(p):
        faces_y(p, (spans[0], spans[-2], spans[-1]))
        inverse(p, spans[:2] + spans[-2:], rim=False)

    over(0, 1, last, plain(lambda p: faces_x(p, (spans[0], spans[-1]))), 0)
    over(1, last - 2, 2, plain(rims), 0)
    begin(field)
    begin(field_later)
    over(2, 1, depth - 4, plain(rims), 0)
    heard(1)
    tell(2)
    arrive(rim_s)
    over(1, 1, depth - 2, plain(rim_field), 0)
    sums = over(2, 1, depth - 4, lambda p, c: first_apply(p, c, spans[:3] + spans[-3:]), sums)

    over(0, 1, 2, plain(own_weights), 0)
    h = over(3, 1, depth - 6, second_apply, zero)
    arrive(face_d)
    arrive(corner_d)
    for edge, first, there in ((0, i == 0, 0), (nx - 1, i == nx - 1, depth + 2)):
        @pl.when(first)
        def _():
            near = there + 1 if edge == 0 else there
            den[near, TOP - 8 : end + 8] = jnp.zeros((width + 16, lanes), F32)
    for bound, first, rows in ((0, j == 0, TOP - 8), (ny - 1, j == ny - 1, end)):
        @pl.when(first)
        def _():
            den[0:2, rows : rows + 8] = jnp.zeros((2, 8, lanes), F32)
            den[depth + 2 : depth + 4, rows : rows + 8] = jnp.zeros((2, 8, lanes), F32)

    arrive(corner_s)
    over(0, 1, 2, plain(own_field), 0)
    sums = over(1, last - 2, 2, first_apply, sums)
    over(0, 1, 2, plain(end_weights), 0)
    h = over(2, depth - 5, 2, second_apply, h)

    arrive(face_s)
    arrive(second_d)
    g0, d0, ss = over(0, 1, 2, end_field, sums)
    h = over(0, 1, 2, end_second, h)
    h = over(1, last - 2, 2, second_apply, h)

    arrive(field)
    low_half, high_half = mids[: half // 16], mids[half // 16 :]
    h = end_last(1, low_half, end_last(0, high_half, h))

    group = lax.broadcasted_iota(jnp.int32, (1, 128), 1) // 32
    row = jnp.zeros((1, 128), F32)
    for k, part in enumerate((g0, d0, ss, h)):
        v = jnp.sum(part, axis=0, keepdims=True)
        v = v + pltpu.roll(v, 64, 1)
        v = v + pltpu.roll(v, 32, 1)
        row = jnp.where(group == k, v, row)

    def spread(k, value, peers, got):
        msg[k] = value
        for s, peer in enumerate(peers):
            pltpu.make_async_remote_copy(
                src_ref=msg.at[k], dst_ref=got.at[s], send_sem=sum_send.at[k], recv_sem=sum_recv.at[k],
                device_id=peer, device_id_type=MESH).start()

    def gathered(k, value, got):
        pltpu.make_async_copy(got, got, sum_recv.at[k]).wait()
        for s in range(got.shape[0]):
            value = value + got[s]
        return value

    spread(0, row, row_peers, got_y)

    def scales(p):
        for r, n in mids:
            rows = pl.ds(r - TOP, n)
            half = 0.5 * inv[p + 1, pl.ds(r, n)]
            scale = half * lax.rsqrt(half)
            scale_out[p, rows] = scale
            t0_out[p, rows] = scale * src[p + 1, pl.ds(r, n)]
            t1_out[p, rows] = scale * t1_out[p, rows]
            t2_out[p, rows] = scale * t2_out[p, rows]

    arrive(field_later)
    end_last(0, low_half, None)
    end_last(1, high_half, None)
    over(0, 1, depth, plain(scales), 0)
    row = gathered(0, row, got_y)
    heard(2)
    spread(1, row, col_peers, got_x)
    for copy, there, _ in copies:
        pl.when(there)(copy.wait_send)
    row = gathered(1, row, got_x)
    pltpu.make_async_copy(got_y, got_y, sum_send.at[0]).wait()
    pltpu.make_async_copy(got_x, got_x, sum_send.at[1]).wait()

    def total(k):
        return jnp.broadcast_to(jnp.sum(jnp.where(group == k, row, 0.0), axis=1, keepdims=True), (1, 128))

    g0, d0, ss, h = (total(k) for k in range(4))
    alpha0 = g0 / d0
    gamma1 = g0 - 2.0 * alpha0 * d0 + alpha0 * alpha0 * ss
    delta1 = d0 - 2.0 * alpha0 * ss + alpha0 * alpha0 * h
    beta1 = gamma1 / g0
    alpha1 = gamma1 / (delta1 - beta1 * gamma1 / alpha0)
    coef_out[0:1] = alpha0 + alpha1 * (1.0 + beta1)
    coef_out[1:2] = alpha0 * alpha1


def combine(t0, t1, t2, scale, coef, pressure, residual, held_p, held_r, sem):
    a, b = coef[0:1, 0:1], coef[1:2, 0:1]
    copies = []
    for p in range(t0.shape[0]):
        u0, u1 = t0[p], t1[p]
        held_p[p] = scale[p] * (a * u0 - b * u1)
        held_r[p] = u0 - a * u1 + b * t2[p]
        for k, (held, out) in enumerate(((held_p, pressure), (held_r, residual))):
            copies.append(pltpu.make_async_copy(held.at[p], out.at[p], sem.at[k, p]))
            copies[-1].start()
    for copy in copies:
        copy.wait()


def solution(mesh):
    sizes = (mesh.shape["gx"], mesh.shape["gy"])

    def shards(source, density):
        depth, width, lanes = source.shape
        shape = jax.ShapeDtypeStruct(source.shape, F32)

        def planes(n):
            return pltpu.VMEM((n, TOP + width + 16, lanes), F32)

        vmem = pl.BlockSpec(memory_space=pltpu.VMEM)
        hbm = pl.BlockSpec(memory_space=pltpu.HBM)
        t0, t1, t2, scale, coef = pl.pallas_call(
            functools.partial(kernel, sizes),
            out_shape=(shape,) * 4 + (jax.ShapeDtypeStruct((2, 128), F32),),
            in_specs=[hbm] * 2,
            out_specs=(vmem,) * 5,
            scratch_shapes=[
                planes(depth + 4), planes(depth + 2), planes(depth + 4), planes(depth + 2),
                planes(depth + 2), planes(depth + 3), planes(depth + 2), planes(depth + 2),
                pltpu.VMEM((2, 1, 128), F32),
                pltpu.VMEM((2 * sizes[1] - 1, 1, 128), F32),
                pltpu.VMEM((sizes[0] // 2 - 1, 1, 128), F32),
                pltpu.SemaphoreType.DMA((2,)),
                pltpu.SemaphoreType.DMA((22,)),
                pltpu.SemaphoreType.DMA((22,)),
                pltpu.SemaphoreType.DMA((2,)),
                pltpu.SemaphoreType.DMA((2,)),
                pltpu.SemaphoreType.REGULAR((3,)),
            ],
            compiler_params=pltpu.CompilerParams(
                collective_id=1, has_side_effects=True, vmem_limit_bytes=36 * 1024 * 1024),
        )(pltpu.with_memory_space_constraint(source, pltpu.HBM), pltpu.with_memory_space_constraint(density, pltpu.HBM))
        pressure, residual = pl.pallas_call(
            combine,
            out_shape=(shape, shape),
            in_specs=[vmem] * 5,
            out_specs=(hbm, hbm),
            scratch_shapes=[
                pltpu.VMEM(source.shape, F32), pltpu.VMEM(source.shape, F32), pltpu.SemaphoreType.DMA((2, depth))],
            compiler_params=pltpu.CompilerParams(vmem_limit_bytes=16 * 1024 * 1024),
        )(t0, t1, t2, scale, coef)
        return pressure, residual

    spec = P("gx", "gy", None)
    return jax.shard_map(shards, mesh=mesh, in_specs=(spec, spec), out_specs=(spec, spec), check_vma=False)
```
